256 devices in a mesh: gx: 64 (over y, z, core), gy: 4 (over x).
Axes of the slice: x: 4, y: 4, z: 8, core: 2. Of those that a mesh axis runs over, the one named last changes fastest.
Arguments:
- pressure: float32 [1024, 256, 256], P('gx', 'gy'), may hold values from -6 to 6
- previous: float32 [1024, 256, 256], P('gx', 'gy'), may hold values from -6 to 6
- oxygen_aux: float32 [1024, 256, 256], P('gx', 'gy'), may hold values from -3 to 3
- nitrogen_aux: float32 [1024, 256, 256], P('gx', 'gy'), may hold values from -3 to 3
- cell_class: int32 [1024, 256, 256], P('gx', 'gy'), may hold values from 0 to 7, as said below
- wall_admittance: float32 [8], replicated, may hold values from 0.1 to 1
- medium: float32 [5], replicated, may hold values from 0.3 to 0.9
Outputs:
- pressure_out: float32 [1024, 256, 256], P('gx', 'gy')
- previous_out: float32 [1024, 256, 256], P('gx', 'gy')
- oxygen_out: float32 [1024, 256, 256], P('gx', 'gy')
- nitrogen_out: float32 [1024, 256, 256], P('gx', 'gy')
The draws below stay inside these ranges and needn't reach their ends.
Inputs may be any that keep to these rules, and one draw needn't show every extreme that they name: `cell_class`: class 0 is air; other classes index wall_admittance.
All inputs are finite; a program needn't handle non-finite values.
Results may differ from the reference program's by a relative error of at most 0.00002.
Values sent between devices are 32-bit elements; how exact they have to be, the bound alone decides.
A program may use at most 64 MiB of HBM per device.

```python
import math
import jax
import jax.numpy as jnp

STEPS = 4
NCLASS = 8
NX = 1024
NY = 256
NZ = 256


def draw_cell_class(key, part):
    key = jax.random.fold_in(key, 7)
    first, second = jax.random.split(key)
    walls = jax.random.randint(first, (NX, NY, NZ), 0, 4)
    kinds = jax.random.randint(second, (NX, NY, NZ), 1, NCLASS)
    return jnp.where(walls == 0, kinds, 0).astype(jnp.int32)


def block_scale(own_key, dims, shards, least, high):
    def one(axis_at, shards_of):
        steps = jax.random.uniform(jax.random.fold_in(jax.random.fold_in(own_key, 6), axis_at), (shards_of,), jnp.float32, least / len(shards), high / len(shards))
        return jnp.repeat(jnp.exp(steps), dims[axis_at] // shards_of).reshape((-1,) + (1,) * (len(dims) - axis_at - 1))

    level = one(*shards[0])
    for cut in shards[1:]:
        level = level * one(*cut)
    return level


def bell_draw(key, shape, width, most, cuts=(), kind=jnp.bfloat16):
    entries = width * jax.random.normal(key, shape, jnp.float32)
    if cuts:
        entries = entries * block_scale(key, shape, cuts, -0.22, 0.18)
    return jnp.clip(entries, -most, most).astype(kind)


def setup_inputs(seed: int = 0) -> dict:
    streams_of = jax.random.split(jax.random.key(seed), 8)
    return {
        "pressure": bell_draw(streams_of[0], (NX, NY, NZ), 1.0, 6.0, ((0, 64), (1, 4)), jnp.float32),
        "previous": bell_draw(streams_of[1], (NX, NY, NZ), 1.0, 6.0, ((0, 64), (1, 4)), jnp.float32),
        "oxygen_aux": bell_draw(streams_of[2], (NX, NY, NZ), 0.5, 3.0, ((0, 64), (1, 4)), jnp.float32),
        "nitrogen_aux": bell_draw(streams_of[3], (NX, NY, NZ), 0.5, 3.0, ((0, 64), (1, 4)), jnp.float32),
        "cell_class": draw_cell_class(jax.random.fold_in(streams_of[7], 71), 0),
        "wall_admittance": jnp.clip(jnp.exp(jax.random.uniform(streams_of[5], (NCLASS,), jnp.float32, math.log(0.1), math.log(1.0))), 0.1, 1.0),
        "medium": jnp.clip(jax.random.uniform(streams_of[6], (5,), jnp.float32, 0.3, 0.9), 0.3, 0.9),
    }


def laplace(field):
    padded = jnp.pad(field, 1)
    total = padded[2:, 1:-1, 1:-1] + padded[:-2, 1:-1, 1:-1]
    total = total + padded[1:-1, 2:, 1:-1] + padded[1:-1, :-2, 1:-1]
    total = total + padded[1:-1, 1:-1, 2:] + padded[1:-1, 1:-1, :-2]
    return total - 6.0 * field


def reference(pressure, previous, oxygen_aux, nitrogen_aux, cell_class, wall_admittance, medium):
    damping = jnp.where(cell_class > 0, wall_admittance[cell_class], jnp.float32(0.0))
    boundary = 0.5 * damping
    for step in range(STEPS):
        change = pressure - previous
        oxygen_aux = medium[0] * oxygen_aux + medium[1] * change
        nitrogen_aux = medium[2] * nitrogen_aux + medium[3] * change
        update = 2.0 * pressure - (1.0 - boundary) * previous + 0.33 * laplace(pressure)
        update = update + (0.05 * medium[4]) * laplace(change) - oxygen_aux - nitrogen_aux
        previous = pressure
        pressure = update / (1.0 + boundary)
    return pressure, previous, oxygen_aux, nitrogen_aux
```

```python
import functools

import jax
import jax.numpy as jnp
from jax import lax
from jax.experimental import pallas as pl
from jax.experimental.pallas import tpu as pltpu
from jax.sharding import PartitionSpec as P

STEPS = 4
NCLASS = 8
MESH = pl.DeviceIdType.MESH
LANES = 128
PAD = 8


def steps_kernel(nx, ny, p_hbm, q_hbm, o_hbm, n_hbm, c_hbm, wall, medium, A, B, O, N,
                 cls, adm, even, odd, gs, ys, yg, cs, xr, yr, yrg, cr,
                 load_sem, send_sem, recv_sem):
    X, H, Y, _ = A.shape
    T = Y // 8
    gx, gy = lax.axis_index("gx"), lax.axis_index("gy")
    xs = (lax.rem(gx + nx - 1, nx), lax.rem(gx + 1, nx))
    yside = (lax.rem(gy + ny - 1, ny), lax.rem(gy + 1, ny))
    barrier = pltpu.get_barrier_semaphore()
    others = [(xs[0], gy), (xs[1], gy), (gx, yside[0]), (gx, yside[1])]
    others += [(xs[i], yside[j]) for i in range(2) for j in range(2)]
    for other in others:
        pl.semaphore_signal(barrier, inc=1, device_id=other, device_id_type=MESH)

    loads = {}
    for at, (name, src, dst) in enumerate(
        (("p", p_hbm, A), ("q", q_hbm, B), ("c", c_hbm, cls), ("o", o_hbm, O), ("n", n_hbm, N))
    ):
        loads[name] = [
            pltpu.make_async_copy(src.at[:, :, pl.ds(LANES * h, LANES)], dst.at[:, h], load_sem.at[at, h])
            for h in range(H)
        ]
        for copy in loads[name]:
            copy.start()

    m0, m1, m2, m3 = medium[0], medium[1], medium[2], medium[3]
    c = 0.05 * medium[4]
    al = 0.33 + c
    inside = [gx > 0, gx < nx - 1]
    mx = [jnp.where(inside[s], 1.0, 0.0).astype(jnp.float32) for s in range(2)]
    my = [jnp.where(t, 1.0, 0.0).astype(jnp.float32) for t in (gy > 0, gy < ny - 1)]

    lane = lax.broadcasted_iota(jnp.int32, (8, LANES), 1)
    first, last = lane == 0, lane == LANES - 1
    zero = jnp.zeros((8, LANES), jnp.float32)

    def rows(j):
        return pl.ds(8 * j, 8)

    def wrows(j, by=0):
        return pl.ds(PAD + 8 * j + by, 8)

    def edge_rows(s):
        return 0 if s == 0 else Y - 1

    def tile(x, j, now, then, src, dst, keep=None):
        w = [src[x + 1, h, wrows(j), :] for h in range(H)]
        down = [pltpu.roll(v, 1, 1) for v in w]
        up = [pltpu.roll(v, LANES - 1, 1) for v in w]
        below = [jnp.where(first, 0.0, down[0]), jnp.where(first, down[0], down[1])]
        above = [jnp.where(last, up[1], up[0]), jnp.where(last, 0.0, up[1])]
        for h in range(H):
            p, q = now[x, h, rows(j), :], then[x, h, rows(j), :]
            total = src[x, h, wrows(j), :] + src[x + 2, h, wrows(j), :]
            total = total + (src[x + 1, h, wrows(j, -1), :] + src[x + 1, h, wrows(j, 1), :])
            total = total + (below[h] + above[h])
            d = p - q
            o = m0 * O[x, h, rows(j), :] + m1 * d
            n = m2 * N[x, h, rows(j), :] + m3 * d
            new = q + adm[x, h, rows(j), :] * ((total - 6.0 * w[h]) + (2.0 * d - (o + n)))
            v = al * new - c * p
            then[x, h, rows(j), :] = new
            O[x, h, rows(j), :] = o
            N[x, h, rows(j), :] = n
            dst[x + 1, h, wrows(j), :] = v
            if keep is not None:
                gs[keep, h, rows(j), :] = v

    def loop(count, body, unroll=1):
        lax.fori_loop(0, count, lambda i, carry: (body(i), carry)[1], 0, unroll=unroll)

    flat_even = even.reshape((X + 2) * H * (Y + 2 * PAD), LANES)
    flat_odd = odd.reshape((X + 2) * H * (Y + 2 * PAD), LANES)
    flat_a = adm.reshape(X * H * Y, LANES)
    flat_b = B.reshape(X * H * Y, LANES)

    def wline(h, y):
        step = H * (Y + 2 * PAD)
        return pl.ds(step + h * (Y + 2 * PAD) + PAD + y, X, stride=step)

    def line(h, y):
        return pl.ds(h * Y + y, X, stride=H * Y)

    def send(at, src, dst, device):
        copy = pltpu.make_async_remote_copy(
            src_ref=src, dst_ref=dst, send_sem=send_sem.at[at], recv_sem=recv_sem.at[at],
            device_id=device, device_id_type=MESH)
        copy.start()
        return copy

    def clear(x):
        for h in range(H):
            even[x, h, pl.ds(0, PAD), :] = zero
            even[x, h, pl.ds(PAD + Y, PAD), :] = zero

    loop(X + 2, clear)

    def clear_planes(j):
        for x in (0, X + 1):
            for h in range(H):
                even[x, h, wrows(j), :] = zero

    loop(T, clear_planes)

    for name in ("p", "q"):
        for copy in loads[name]:
            copy.wait()

    def first_w(x):
        for j in range(T):
            for h in range(H):
                even[x + 1, h, wrows(j), :] = al * A[x, h, rows(j), :] - c * B[x, h, rows(j), :]

    loop(X, first_w)

    table = [1.0 / (1.0 + 0.5 * jnp.full((8, LANES), wall[k], jnp.float32)) for k in range(1, NCLASS)]
    for copy in loads["c"]:
        copy.wait()

    def admit(x):
        for j in range(T):
            for h in range(H):
                kind = cls[x, h, rows(j), :]
                a = jnp.ones((8, LANES), jnp.float32)
                for k in range(1, NCLASS):
                    a = jnp.where(kind == k, table[k - 1], a)
                adm[x, h, rows(j), :] = a

    loop(X, admit)

    pending = {}
    message = iter(range(64))
    pl.semaphore_wait(barrier, len(others))

    def send_planes(e):
        for s in range(2):
            pending["w", e, s] = send(
                next(message), even.at[1 if s == 0 else X, :, pl.ds(PAD, Y), :], xr.at[e, 0, 1 - s], (xs[s], gy))

    def send_corners(e):
        for s in range(2):
            for t in range(2):
                for h in range(H):
                    cs[e, s, t, pl.ds(h, 1), :] = even[1 if s == 0 else X, h, pl.ds(PAD + edge_rows(t), 1), :]
                pending["c", e, s, t] = send(
                    next(message), cs.at[e, s, t], cr.at[e, 1 - s, 1 - t], (xs[s], yside[t]))

    def send_lines(e):
        for t in range(2):
            for h in range(H):
                ys[e, t, 0, h] = flat_even[wline(h, edge_rows(t)), :]
                if e == 0:
                    ys[e, t, 1, h] = flat_a[line(h, edge_rows(t)), :]
            fields = 2 if e == 0 else 1
            pending["y", e, t] = send(
                next(message), ys.at[e, t, pl.ds(0, fields)], yr.at[e, 1 - t, pl.ds(0, fields)], (gx, yside[t]))

    for e in range(STEPS // 2):
        if e == 0:
            send_planes(e)
            send_lines(e)
            send_corners(e)
            for s in range(2):
                pending["a", s] = send(
                    next(message), adm.at[0 if s == 0 else X - 1], xr.at[0, 2, 1 - s], (xs[s], gy))
            for name in ("o", "n"):
                for copy in loads[name]:
                    copy.wait()

        def first_planes(i, e=e):
            for j in range(T):
                tile((X - 1) * i, j, A, B, even, odd, keep=2 * e + i)

        loop(2, first_planes)
        for s in range(2):
            pending["g", e, s] = send(next(message), gs.at[2 * e + s], xr.at[e, 1, 1 - s], (xs[s], gy))

        if e > 0:
            def rest(i):
                for j in (0, T - 1):
                    tile(i + 2, j, B, A, odd, even)

            loop(X - 4, rest, 2)
            send_lines(e)

        def plane(i):
            for j in range(T):
                tile(i + 1, j, A, B, even, odd)

        loop(X - 2, plane, 2)
        for t in range(2):
            for h in range(H):
                yg[e, t, h] = flat_odd[wline(h, edge_rows(t)), :]
            pending["yg", e, t] = send(next(message), yg.at[e, t], yrg.at[e, 1 - t], (gx, yside[t]))

        def inner(i):
            for j in range(1, T - 1):
                tile(i + 2, j, B, A, odd, even)

        loop(X - 4, inner, 2)

        for t in range(2):
            pending["y", e, t].wait_recv()
        for t in range(2):
            for h in range(H):
                add = flat_a[line(h, edge_rows(t)), :] * (my[t] * yr[e, t, 0, h])
                flat_b[line(h, edge_rows(t)), :] = flat_b[line(h, edge_rows(t)), :] + add
                flat_odd[wline(h, edge_rows(t)), :] = flat_odd[wline(h, edge_rows(t)), :] + al * add
        for t in range(2):
            pending["yg", e, t].wait_recv()
        for t in range(2):
            for h in range(H):
                y = -1 if t == 0 else Y
                flat_odd[wline(h, y), :] = my[t] * (yrg[e, t, h] + al * yr[0, t, 1, h] * ys[e, t, 0, h])
        for s in range(2):
            pending["w", e, s].wait_recv()
        for s in range(2):
            x = 0 if s == 0 else X - 1

            def face(j, s=s, x=x, e=e):
                for h in range(H):
                    add = adm[x, h, rows(j), :] * (mx[s] * xr[e, 0, s, h, rows(j), :])
                    B[x, h, rows(j), :] = B[x, h, rows(j), :] + add
                    odd[x + 1, h, wrows(j), :] = odd[x + 1, h, wrows(j), :] + al * add

            loop(T, face, T)
        for s in range(2):
            if e == 0:
                pending["a", s].wait_recv()
            pending["g", e, s].wait_recv()
        for s in range(2):
            x, halo = (0, 0) if s == 0 else (X - 1, X + 1)

            def layer(j, s=s, x=x, halo=halo, e=e):
                for h in range(H):
                    odd[halo, h, wrows(j), :] = mx[s] * (
                        xr[e, 1, s, h, rows(j), :]
                        + al * xr[0, 2, s, h, rows(j), :] * even[x + 1, h, wrows(j), :])

            loop(T, layer, T)
        for s in range(2):
            for t in range(2):
                pending["c", e, s, t].wait_recv()
        for s in range(2):
            x, halo = (1, 0) if s == 0 else (X, X + 1)
            for t in range(2):
                y, over = (0, -1) if t == 0 else (Y - 1, Y)
                for h in range(H):
                    scaled = (mx[s] * my[t] * al) * cr[e, s, t, pl.ds(h, 1), :]
                    at = pl.ds(PAD + y, 1)
                    odd[halo, h, at, :] = odd[halo, h, at, :] + xr[0, 2, s, h, pl.ds(y, 1), :] * scaled
                    at = pl.ds(PAD + over, 1)
                    odd[x, h, at, :] = odd[x, h, at, :] + yr[0, t, 1, h, pl.ds(x - 1, 1), :] * scaled
            pending["w", e, s].wait_send()

        def ends(i):
            for j in range(T):
                tile((X - 1) * i, j, B, A, odd, even)

        loop(2, ends)
        if e == 0:
            send_planes(1)
            send_corners(1)

        def next_ends(i):
            for j in range(T):
                tile(1 + (X - 3) * i, j, B, A, odd, even)

        loop(2, next_ends)
        if e > 0:
            def rest_last(i):
                for j in (0, T - 1):
                    tile(i + 2, j, B, A, odd, even)

            loop(X - 4, rest_last, 2)

    for name, copy in pending.items():
        if name[0] != "w":
            copy.wait_send()


def store_kernel(a, b, o, n, p_out, q_out, o_out, n_out, sems):
    copies = [
        pltpu.make_async_copy(src.at[:, h], dst.at[:, :, pl.ds(LANES * h, LANES)], sems.at[at, h])
        for at, (src, dst) in enumerate(((a, p_out), (b, q_out), (o, o_out), (n, n_out)))
        for h in range(2)
    ]
    for copy in copies:
        copy.start()
    for copy in copies:
        copy.wait()


def per_device(nx, ny, pressure, previous, oxygen_aux, nitrogen_aux, cell_class, wall_admittance, medium):
    X, Y, Z = pressure.shape
    H = Z // LANES
    split = (X, H, Y, LANES)
    padded = (X + 2, H, Y + 2 * PAD, LANES)
    hbm = pl.BlockSpec(memory_space=pl.ANY)
    vmem = pl.BlockSpec(memory_space=pltpu.VMEM)
    smem = pl.BlockSpec(memory_space=pltpu.SMEM)
    f32 = jnp.float32
    state = pl.pallas_call(
        functools.partial(steps_kernel, nx, ny),
        out_shape=[pltpu.VMEM(split, f32)] * 4,
        in_specs=[hbm] * 5 + [smem] * 2,
        out_specs=[vmem] * 4,
        scratch_shapes=[
            pltpu.VMEM(split, jnp.int32),
            pltpu.VMEM(split, f32),
            pltpu.VMEM(padded, f32),
            pltpu.VMEM(padded, f32),
            pltpu.VMEM((4, H, Y, LANES), f32),
            pltpu.VMEM((2, 2, 2, H, X, LANES), f32),
            pltpu.VMEM((2, 2, H, X, LANES), f32),
            pltpu.VMEM((2, 2, 2, 8, LANES), f32),
            pltpu.VMEM((2, 3, 2, H, Y, LANES), f32),
            pltpu.VMEM((2, 2, 2, H, X, LANES), f32),
            pltpu.VMEM((2, 2, H, X, LANES), f32),
            pltpu.VMEM((2, 2, 2, 8, LANES), f32),
            pltpu.SemaphoreType.DMA((5, 2)),
            pltpu.SemaphoreType.DMA((32,)),
            pltpu.SemaphoreType.DMA((32,)),
        ],
        compiler_params=pltpu.CompilerParams(
            collective_id=0, has_side_effects=True, vmem_limit_bytes=56 << 20),
    )(pressure, previous, oxygen_aux, nitrogen_aux, cell_class, wall_admittance, medium)
    out = pl.pallas_call(
        store_kernel,
        out_shape=[jax.ShapeDtypeStruct((X, Y, Z), f32)] * 4,
        in_specs=[vmem] * 4,
        out_specs=[hbm] * 4,
        scratch_shapes=[pltpu.SemaphoreType.DMA((4, 2))],
        compiler_params=pltpu.CompilerParams(vmem_limit_bytes=16 << 20),
    )(*state)
    return tuple(out)


def solution(mesh):
    field = P("gx", "gy", None)
    return jax.shard_map(
        functools.partial(per_device, mesh.shape["gx"], mesh.shape["gy"]),
        mesh=mesh,
        in_specs=(field,) * 5 + (P(), P()),
        out_specs=(field,) * 4,
        check_vma=False,
    )
```

```python
import functools

import jax
import jax.numpy as jnp
from jax import lax
from jax.experimental import pallas as pl
from jax.experimental.pallas import tpu as pltpu
from jax.sharding import PartitionSpec as P

STEPS = 4
NCLASS = 8
MESH = pl.DeviceIdType.MESH
LANES = 128
PAD = 8


def steps_kernel(nx, ny, p_hbm, q_hbm, o_hbm, n_hbm, c_hbm, wall, medium, A, B, O, N,
                 cls, adm, even, odd, gs, ys, yg, cs, xr, yr, yrg, cr,
                 load_sem, send_sem, recv_sem):
    X, H, Y, _ = A.shape
    T = Y // 8
    gx, gy = lax.axis_index("gx"), lax.axis_index("gy")
    xs = (lax.rem(gx + nx - 1, nx), lax.rem(gx + 1, nx))
    yside = (lax.rem(gy + ny - 1, ny), lax.rem(gy + 1, ny))
    barrier = pltpu.get_barrier_semaphore()
    others = [(xs[0], gy), (xs[1], gy), (gx, yside[0]), (gx, yside[1])]
    others += [(xs[i], yside[j]) for i in range(2) for j in range(2)]
    there_x = (gx > 0, gx < nx - 1)
    there_y = (gy > 0, gy < ny - 1)
    there = [there_x[0], there_x[1], there_y[0], there_y[1]]
    there += [there_x[i] & there_y[j] for i in range(2) for j in range(2)]
    for other, ok in zip(others, there):
        @pl.when(ok)
        def _():
            pl.semaphore_signal(barrier, inc=1, device_id=other, device_id_type=MESH)

    loads = {}
    for at, (name, src, dst) in enumerate(
        (("p", p_hbm, A), ("q", q_hbm, B), ("c", c_hbm, cls), ("o", o_hbm, O), ("n", n_hbm, N))
    ):
        loads[name] = [
            pltpu.make_async_copy(src.at[:, :, pl.ds(LANES * h, LANES)], dst.at[:, h], load_sem.at[at, h])
            for h in range(H)
        ]
        for copy in loads[name]:
            copy.start()

    m0, m1, m2, m3 = medium[0], medium[1], medium[2], medium[3]
    c = 0.05 * medium[4]
    al = 0.33 + c

    lane = lax.broadcasted_iota(jnp.int32, (8, LANES), 1)
    first, last = lane == 0, lane == LANES - 1
    zero = jnp.zeros((8, LANES), jnp.float32)

    def rows(j):
        return pl.ds(8 * j, 8)

    def wrows(j, by=0):
        return pl.ds(PAD + 8 * j + by, 8)

    def edge_rows(s):
        return 0 if s == 0 else Y - 1

    def tile(x, j, now, then, src, dst, keep=None):
        w = [src[x + 1, h, wrows(j), :] for h in range(H)]
        down = [pltpu.roll(v, 1, 1) for v in w]
        up = [pltpu.roll(v, LANES - 1, 1) for v in w]
        below = [jnp.where(first, 0.0, down[0]), jnp.where(first, down[0], down[1])]
        above = [jnp.where(last, up[1], up[0]), jnp.where(last, 0.0, up[1])]
        for h in range(H):
            p, q = now[x, h, rows(j), :], then[x, h, rows(j), :]
            total = src[x, h, wrows(j), :] + src[x + 2, h, wrows(j), :]
            total = total + (src[x + 1, h, wrows(j, -1), :] + src[x + 1, h, wrows(j, 1), :])
            total = total + (below[h] + above[h])
            d = p - q
            o = m0 * O[x, h, rows(j), :] + m1 * d
            n = m2 * N[x, h, rows(j), :] + m3 * d
            new = q + adm[x, h, rows(j), :] * ((total - 6.0 * w[h]) + (2.0 * d - (o + n)))
            v = al * new - c * p
            then[x, h, rows(j), :] = new
            O[x, h, rows(j), :] = o
            N[x, h, rows(j), :] = n
            dst[x + 1, h, wrows(j), :] = v
            if keep is not None:
                gs[keep, h, rows(j), :] = v

    def loop(count, body, unroll=1):
        lax.fori_loop(0, count, lambda i, carry: (body(i), carry)[1], 0, unroll=unroll)

    flat_even = even.reshape((X + 2) * H * (Y + 2 * PAD), LANES)
    flat_odd = odd.reshape((X + 2) * H * (Y + 2 * PAD), LANES)
    flat_a = adm.reshape(X * H * Y, LANES)
    flat_b = B.reshape(X * H * Y, LANES)

    def wline(h, y):
        step = H * (Y + 2 * PAD)
        return pl.ds(step + h * (Y + 2 * PAD) + PAD + y, X, stride=step)

    def line(h, y):
        return pl.ds(h * Y + y, X, stride=H * Y)

    def send(at, src, dst, device, ok, back):
        def describe():
            return pltpu.make_async_remote_copy(
                src_ref=src, dst_ref=dst, send_sem=send_sem.at[at], recv_sem=recv_sem.at[at],
                device_id=device, device_id_type=MESH)

        @pl.when(ok)
        def _():
            describe().start()

        return describe, ok, back

    def sent(entry):
        describe, ok, _ = entry

        @pl.when(ok)
        def _():
            describe().wait_send()

    def arrived(entry):
        describe, _, back = entry

        @pl.when(back)
        def _():
            describe().wait_recv()

    def clear(x):
        for h in range(H):
            even[x, h, pl.ds(0, PAD), :] = zero
            even[x, h, pl.ds(PAD + Y, PAD), :] = zero

    loop(X + 2, clear)

    def clear_planes(j):
        for x in (0, X + 1):
            for h in range(H):
                even[x, h, wrows(j), :] = zero

    loop(T, clear_planes)

    for name in ("p", "q"):
        for copy in loads[name]:
            copy.wait()

    def first_w(x):
        for j in range(T):
            for h in range(H):
                even[x + 1, h, wrows(j), :] = al * A[x, h, rows(j), :] - c * B[x, h, rows(j), :]

    loop(X, first_w)

    table = [1.0 / (1.0 + 0.5 * jnp.full((8, LANES), wall[k], jnp.float32)) for k in range(1, NCLASS)]
    for copy in loads["c"]:
        copy.wait()

    def admit(x):
        for j in range(T):
            for h in range(H):
                kind = cls[x, h, rows(j), :]
                a = jnp.ones((8, LANES), jnp.float32)
                for k in range(1, NCLASS):
                    a = jnp.where(kind == k, table[k - 1], a)
                adm[x, h, rows(j), :] = a

    loop(X, admit)

    for s in range(2):
        @pl.when(jnp.logical_not(there_x[s]))
        def _():
            def none(j):
                for h in range(H):
                    xr[0, 2, s, h, rows(j), :] = zero
                    for e in range(2):
                        for field in range(2):
                            xr[e, field, s, h, rows(j), :] = zero

            loop(T, none)

        @pl.when(jnp.logical_not(there_y[s]))
        def _():
            blank = jnp.zeros((X, LANES), jnp.float32)
            for h in range(H):
                yr[0, s, 1, h] = blank
                for e in range(2):
                    yr[e, s, 0, h] = blank
                    yrg[e, s, h] = blank

        for t in range(2):
            @pl.when(jnp.logical_not(there_x[s] & there_y[t]))
            def _():
                for e in range(2):
                    cr[e, s, t] = zero

    pending = {}
    message = iter(range(64))
    beside_x = jnp.where(gx > 0, 1, 0) + jnp.where(gx < nx - 1, 1, 0)
    beside_y = jnp.where(gy > 0, 1, 0) + jnp.where(gy < ny - 1, 1, 0)
    pl.semaphore_wait(barrier, beside_x + beside_y + beside_x * beside_y)

    def send_planes(e):
        for s in range(2):
            pending["w", e, s] = send(
                next(message), even.at[1 if s == 0 else X, :, pl.ds(PAD, Y), :], xr.at[e, 0, 1 - s], (xs[s], gy), there_x[s], there_x[1 - s])

    def send_corners(e):
        for s in range(2):
            for t in range(2):
                for h in range(H):
                    cs[e, s, t, pl.ds(h, 1), :] = even[1 if s == 0 else X, h, pl.ds(PAD + edge_rows(t), 1), :]
                pending["c", e, s, t] = send(
                    next(message), cs.at[e, s, t], cr.at[e, 1 - s, 1 - t], (xs[s], yside[t]), there_x[s] & there_y[t], there_x[1 - s] & there_y[1 - t])

    def send_lines(e):
        for t in range(2):
            for h in range(H):
                ys[e, t, 0, h] = flat_even[wline(h, edge_rows(t)), :]
                if e == 0:
                    ys[e, t, 1, h] = flat_a[line(h, edge_rows(t)), :]
            fields = 2 if e == 0 else 1
            pending["y", e, t] = send(
                next(message), ys.at[e, t, pl.ds(0, fields)], yr.at[e, 1 - t, pl.ds(0, fields)], (gx, yside[t]), there_y[t], there_y[1 - t])

    for e in range(STEPS // 2):
        if e == 0:
            send_planes(e)
            send_lines(e)
            send_corners(e)
            for s in range(2):
                pending["a", s] = send(
                    next(message), adm.at[0 if s == 0 else X - 1], xr.at[0, 2, 1 - s], (xs[s], gy), there_x[s], there_x[1 - s])
            for name in ("o", "n"):
                for copy in loads[name]:
                    copy.wait()

        def first_planes(i, e=e):
            for j in range(T):
                tile((X - 1) * i, j, A, B, even, odd, keep=2 * e + i)

        loop(2, first_planes)
        for s in range(2):
            pending["g", e, s] = send(next(message), gs.at[2 * e + s], xr.at[e, 1, 1 - s], (xs[s], gy), there_x[s], there_x[1 - s])

        if e > 0:
            def rest(i):
                for j in (0, T - 1):
                    tile(i + 2, j, B, A, odd, even)

            loop(X - 4, rest, 2)
            send_lines(e)

        def plane(i):
            for j in range(T):
                tile(i + 1, j, A, B, even, odd)

        loop(X - 2, plane, 2)
        for t in range(2):
            for h in range(H):
                yg[e, t, h] = flat_odd[wline(h, edge_rows(t)), :]
            pending["yg", e, t] = send(next(message), yg.at[e, t], yrg.at[e, 1 - t], (gx, yside[t]), there_y[t], there_y[1 - t])

        def inner(i):
            for j in range(1, T - 1):
                tile(i + 2, j, B, A, odd, even)

        loop(X - 4, inner, 2)

        for t in range(2):
            arrived(pending["y", e, t])
        for t in range(2):
            for h in range(H):
                add = flat_a[line(h, edge_rows(t)), :] * yr[e, t, 0, h]
                flat_b[line(h, edge_rows(t)), :] = flat_b[line(h, edge_rows(t)), :] + add
                flat_odd[wline(h, edge_rows(t)), :] = flat_odd[wline(h, edge_rows(t)), :] + al * add
        for t in range(2):
            arrived(pending["yg", e, t])
        for t in range(2):
            for h in range(H):
                y = -1 if t == 0 else Y
                flat_odd[wline(h, y), :] = yrg[e, t, h] + al * yr[0, t, 1, h] * ys[e, t, 0, h]
        for s in range(2):
            arrived(pending["w", e, s])
        for s in range(2):
            x = 0 if s == 0 else X - 1

            def face(j, s=s, x=x, e=e):
                for h in range(H):
                    add = adm[x, h, rows(j), :] * xr[e, 0, s, h, rows(j), :]
                    B[x, h, rows(j), :] = B[x, h, rows(j), :] + add
                    odd[x + 1, h, wrows(j), :] = odd[x + 1, h, wrows(j), :] + al * add

            loop(T, face, T)
        for s in range(2):
            if e == 0:
                arrived(pending["a", s])
            arrived(pending["g", e, s])
        for s in range(2):
            x, halo = (0, 0) if s == 0 else (X - 1, X + 1)

            def layer(j, s=s, x=x, halo=halo, e=e):
                for h in range(H):
                    odd[halo, h, wrows(j), :] = (
                        xr[e, 1, s, h, rows(j), :]
                        + al * xr[0, 2, s, h, rows(j), :] * even[x + 1, h, wrows(j), :])

            loop(T, layer, T)
        for s in range(2):
            for t in range(2):
                arrived(pending["c", e, s, t])
        for s in range(2):
            x, halo = (1, 0) if s == 0 else (X, X + 1)
            for t in range(2):
                y, over = (0, -1) if t == 0 else (Y - 1, Y)
                for h in range(H):
                    scaled = al * cr[e, s, t, pl.ds(h, 1), :]
                    at = pl.ds(PAD + y, 1)
                    odd[halo, h, at, :] = odd[halo, h, at, :] + xr[0, 2, s, h, pl.ds(y, 1), :] * scaled
                    at = pl.ds(PAD + over, 1)
                    odd[x, h, at, :] = odd[x, h, at, :] + yr[0, t, 1, h, pl.ds(x - 1, 1), :] * scaled
            sent(pending["w", e, s])

        def ends(i):
            for j in range(T):
                tile((X - 1) * i, j, B, A, odd, even)

        loop(2, ends)
        if e == 0:
            send_planes(1)
            send_corners(1)

        def next_ends(i):
            for j in range(T):
                tile(1 + (X - 3) * i, j, B, A, odd, even)

        loop(2, next_ends)
        if e > 0:
            def rest_last(i):
                for j in (0, T - 1):
                    tile(i + 2, j, B, A, odd, even)

            loop(X - 4, rest_last, 2)

    for name, copy in pending.items():
        if name[0] != "w":
            sent(copy)


def store_kernel(a, b, o, n, p_out, q_out, o_out, n_out, sems):
    copies = [
        pltpu.make_async_copy(src.at[:, h], dst.at[:, :, pl.ds(LANES * h, LANES)], sems.at[at, h])
        for at, (src, dst) in enumerate(((a, p_out), (b, q_out), (o, o_out), (n, n_out)))
        for h in range(2)
    ]
    for copy in copies:
        copy.start()
    for copy in copies:
        copy.wait()


def per_device(nx, ny, pressure, previous, oxygen_aux, nitrogen_aux, cell_class, wall_admittance, medium):
    X, Y, Z = pressure.shape
    H = Z // LANES
    split = (X, H, Y, LANES)
    padded = (X + 2, H, Y + 2 * PAD, LANES)
    hbm = pl.BlockSpec(memory_space=pl.ANY)
    vmem = pl.BlockSpec(memory_space=pltpu.VMEM)
    smem = pl.BlockSpec(memory_space=pltpu.SMEM)
    f32 = jnp.float32
    state = pl.pallas_call(
        functools.partial(steps_kernel, nx, ny),
        out_shape=[pltpu.VMEM(split, f32)] * 4,
        in_specs=[hbm] * 5 + [smem] * 2,
        out_specs=[vmem] * 4,
        scratch_shapes=[
            pltpu.VMEM(split, jnp.int32),
            pltpu.VMEM(split, f32),
            pltpu.VMEM(padded, f32),
            pltpu.VMEM(padded, f32),
            pltpu.VMEM((4, H, Y, LANES), f32),
            pltpu.VMEM((2, 2, 2, H, X, LANES), f32),
            pltpu.VMEM((2, 2, H, X, LANES), f32),
            pltpu.VMEM((2, 2, 2, 8, LANES), f32),
            pltpu.VMEM((2, 3, 2, H, Y, LANES), f32),
            pltpu.VMEM((2, 2, 2, H, X, LANES), f32),
            pltpu.VMEM((2, 2, H, X, LANES), f32),
            pltpu.VMEM((2, 2, 2, 8, LANES), f32),
            pltpu.SemaphoreType.DMA((5, 2)),
            pltpu.SemaphoreType.DMA((32,)),
            pltpu.SemaphoreType.DMA((32,)),
        ],
        compiler_params=pltpu.CompilerParams(
            collective_id=0, has_side_effects=True, vmem_limit_bytes=56 << 20),
    )(pressure, previous, oxygen_aux, nitrogen_aux, cell_class, wall_admittance, medium)
    out = pl.pallas_call(
        store_kernel,
        out_shape=[jax.ShapeDtypeStruct((X, Y, Z), f32)] * 4,
        in_specs=[vmem] * 4,
        out_specs=[hbm] * 4,
        scratch_shapes=[pltpu.SemaphoreType.DMA((4, 2))],
        compiler_params=pltpu.CompilerParams(vmem_limit_bytes=16 << 20),
    )(*state)
    return tuple(out)


def solution(mesh):
    field = P("gx", "gy", None)
    return jax.shard_map(
        functools.partial(per_device, mesh.shape["gx"], mesh.shape["gy"]),
        mesh=mesh,
        in_specs=(field,) * 5 + (P(), P()),
        out_specs=(field,) * 4,
        check_vma=False,
    )
```

```python
import functools

import jax
import jax.numpy as jnp
from jax import lax
from jax.experimental import pallas as pl
from jax.experimental.pallas import tpu as pltpu
from jax.sharding import PartitionSpec as P

STEPS = 4
NCLASS = 8
MESH = pl.DeviceIdType.MESH
LANES = 128
PAD = 8
WIDE = 16
OUT = 3


def steps_kernel(nx, ny, p_hbm, q_hbm, o_hbm, n_hbm, c_hbm, wall, medium, A, B, O, N,
                 cls, adm, even, odd, dA, dB, dO, dN, dE, dD,
                 fs, ys, ya, xe, cs0, cs1, fr, xa, yr, yar, xer, cr0, cr1,
                 load_sem, send_sem, recv_sem):
    X, H, Y, _ = A.shape
    T = Y // 8
    gx, gy = lax.axis_index("gx"), lax.axis_index("gy")
    xs = (lax.rem(gx + nx - 1, nx), lax.rem(gx + 1, nx))
    yside = (lax.rem(gy + ny - 1, ny), lax.rem(gy + 1, ny))
    there_x = (gx > 0, gx < nx - 1)
    there_y = (gy > 0, gy < ny - 1)
    sides = [(s, t) for s in range(2) for t in range(2)]

    barrier = pltpu.get_barrier_semaphore()
    others = [((xs[s], gy), there_x[s]) for s in range(2)]
    others += [((gx, yside[t]), there_y[t]) for t in range(2)]
    others += [((xs[s], yside[t]), there_x[s] & there_y[t]) for s, t in sides]
    for other, ok in others:
        @pl.when(ok)
        def _():
            pl.semaphore_signal(barrier, inc=1, device_id=other, device_id_type=MESH)

    loads = {}
    for at, (name, src, dst) in enumerate(
        (("p", p_hbm, A), ("q", q_hbm, B), ("c", c_hbm, cls), ("o", o_hbm, O), ("n", n_hbm, N))
    ):
        loads[name] = [
            pltpu.make_async_copy(src.at[:, :, pl.ds(LANES * h, LANES)], dst.at[:, h], load_sem.at[at, h])
            for h in range(H)
        ]
        for copy in loads[name]:
            copy.start()

    def loaded(name):
        for copy in loads[name]:
            copy.wait()

    m0, m1, m2, m3 = medium[0], medium[1], medium[2], medium[3]
    c = 0.05 * medium[4]
    al = 0.33 + c

    lane = lax.broadcasted_iota(jnp.int32, (8, LANES), 1)
    first, last = lane == 0, lane == LANES - 1
    zero = jnp.zeros((8, LANES), jnp.float32)

    def loop(count, body, unroll=1):
        lax.fori_loop(0, count, lambda i, carry: (body(i), carry)[1], 0, unroll=unroll)

    def rows(j, pad=0, by=0):
        return pl.ds(pad + 8 * j + by, 8)

    def depth_x(s, d):
        return d if s == 0 else X - 1 - d

    def depth_y(t, d):
        return d if t == 0 else Y - 1 - d

    def advance(x, j, now, then, oxy, nit, xo, pad, src, wx, wpad):
        w = [src[x + wx, h, rows(j, wpad), :] for h in range(H)]
        down = [pltpu.roll(v, 1, 1) for v in w]
        up = [pltpu.roll(v, LANES - 1, 1) for v in w]
        below = [jnp.where(first, 0.0, down[0]), jnp.where(first, down[0], down[1])]
        above = [jnp.where(last, up[1], up[0]), jnp.where(last, 0.0, up[1])]
        result = []
        for h in range(H):
            at = (x + xo, h, rows(j, pad), slice(None))
            p, q = now[at], then[at]
            total = src[x + wx - 1, h, rows(j, wpad), :] + src[x + wx + 1, h, rows(j, wpad), :]
            total = total + (src[x + wx, h, rows(j, wpad, -1), :] + src[x + wx, h, rows(j, wpad, 1), :])
            total = total + (below[h] + above[h])
            d = p - q
            o = m0 * oxy[at] + m1 * d
            n = m2 * nit[at] + m3 * d
            new = q + adm[x + OUT, h, rows(j, PAD), :] * ((total - 6.0 * w[h]) + (2.0 * d - (o + n)))
            result.append((h, at, p, new, o, n))
        return result

    def alone(x, tiles, now, then, src, dst, keep=None):
        for j0 in range(0, len(tiles), 2):
            done = [(j, r) for j in tiles[j0:j0 + 2] for r in advance(x, j, now, then, O, N, 0, 0, src, 1, PAD)]
            for j, (h, at, p, new, o, n) in done:
                then[at] = new
                O[at] = o
                N[at] = n
                if dst is not None:
                    v = al * new - c * p
                    dst[x + 1, h, rows(j, PAD), :] = v
                    if keep is not None:
                        keep[h, rows(j), :] = v

    def coupled(x, tiles, now, then, src, dst):
        for j0 in range(0, len(tiles), 2):
            done = [(j, r) for j in tiles[j0:j0 + 2]
                    for r in advance(x, j, now, then, dO, dN, OUT, WIDE, src, OUT, WIDE)]
            for j, (h, at, p, new, o, n) in done:
                if dst is not None:
                    then[at] = new
                    dO[at] = o
                    dN[at] = n
                    dst[at] = al * new - c * p
                else:
                    to = (x, h, rows(j), slice(None))
                    A[to] = A[to] + new
                    B[to] = B[to] + p
                    O[to] = O[to] + o
                    N[to] = N[to] + n

    def flat(ref):
        planes, halves, height, _ = ref.shape
        return ref.reshape(planes * halves * height, LANES)

    def line(ref, h, y, xo, pad):
        height = ref.shape[2]
        return pl.ds((xo * H + h) * height + pad + y, X, stride=H * height)

    messages = iter(range(64))

    def send(src, dst, device, ok, back):
        at = next(messages)

        def describe():
            return pltpu.make_async_remote_copy(
                src_ref=src, dst_ref=dst, send_sem=send_sem.at[at], recv_sem=recv_sem.at[at],
                device_id=device, device_id_type=MESH)

        @pl.when(ok)
        def _():
            describe().start()

        return describe, ok, back

    def sent(entry):
        @pl.when(entry[1])
        def _():
            entry[0]().wait_send()

    def arrived(entry):
        @pl.when(entry[2])
        def _():
            entry[0]().wait_recv()

    def clear(x):
        for ref in (dE, dD, dA, dB, dO, dN):
            for h in range(H):
                for j in range(-2, T + 2):
                    ref[x, h, rows(j, WIDE), :] = zero
        for h in range(H):
            adm[x, h, rows(-1, PAD), :] = zero
            adm[x, h, rows(T, PAD), :] = zero

    def clear_own(x):
        for h in range(H):
            for ref in (even, odd):
                ref[x, h, rows(-1, PAD), :] = zero
                ref[x, h, rows(T, PAD), :] = zero

    def clear_faces(j):
        for h in range(H):
            for ref in (even, odd):
                for x in (0, X + 1):
                    ref[x, h, rows(j, PAD), :] = zero
            for x in (0, X + 2 * OUT - 1):
                adm[x, h, rows(j, PAD), :] = zero

    loop(X + 2 * OUT, clear)
    loop(X + 2, clear_own)
    loop(T, clear_faces)
    blank = jnp.zeros((X, LANES), jnp.float32)
    for s in range(2):
        @pl.when(jnp.logical_not(there_x[s]))
        def _():
            def none(j):
                for h in range(H):
                    for k in range(STEPS):
                        fr[k, s, h, rows(j), :] = zero
                    for d in range(2):
                        xa[s, d, h, rows(j), :] = zero

            loop(T, none)
            xer[s] = zero

        @pl.when(jnp.logical_not(there_y[s]))
        def _():
            for h in range(H):
                for k in range(1, STEPS):
                    yr[k, s, h] = blank
                for f in range(3):
                    yar[s, pl.ds((f * H + h) * X, X), :] = blank
            yar[s, pl.ds(3 * H * X, 8), :] = zero

        for t in range(2):
            @pl.when(jnp.logical_not(there_x[s] & there_y[t]))
            def _():
                cr0[s, t, pl.ds(0, 8), :] = zero
                cr0[s, t, pl.ds(8, 8), :] = zero
                cr1[0, s, t] = zero
                cr1[1, s, t] = zero

    loaded("p")
    loaded("q")

    def first_w(x, keep=None):
        for j in range(T):
            for h in range(H):
                v = al * A[x, h, rows(j), :] - c * B[x, h, rows(j), :]
                even[x + 1, h, rows(j, PAD), :] = v
                if keep is not None:
                    keep[h, rows(j), :] = v

    table = [1.0 / (1.0 + 0.5 * jnp.full((8, LANES), wall[k], jnp.float32)) for k in range(1, NCLASS)]

    def admit(x):
        for j in range(T):
            for h in range(H):
                kind = cls[x, h, rows(j), :]
                a = jnp.ones((8, LANES), jnp.float32)
                for k in range(1, NCLASS):
                    a = jnp.where(kind == k, table[k - 1], a)
                adm[x + OUT, h, rows(j, PAD), :] = a

    loop(2, lambda s: first_w((X - 1) * s, fs.at[0, s]))
    loop(X - 2, lambda i: first_w(i + 1), 2)
    loaded("c")
    loop(X, admit, 2)

    def row(ref, x, h, y, xo, pad):
        return ref[x + xo, h, pl.ds(pad + y, 1), :]

    flat_a = flat(adm)
    for t in range(2):
        for h in range(H):
            ya[t, pl.ds(h * X, X), :] = flat(even)[line(even, h, depth_y(t, 0), 1, PAD), :]
            for d in range(2):
                ya[t, pl.ds(((d + 1) * H + h) * X, X), :] = flat_a[line(adm, h, depth_y(t, d), OUT, PAD), :]
            for s in range(2):
                ya[t, pl.ds(3 * H * X + s * H + h, 1), :] = row(even, depth_x(s, 0), h, depth_y(t, 1), 1, PAD)
                ya[t, pl.ds(3 * H * X + 2 * H + s * H + h, 1), :] = row(
                    adm, depth_x(s, 0), h, depth_y(t, 2), OUT, PAD)
    near = ((0, 0), (1, 0), (0, 1), (2, 0), (0, 2))
    for s in range(2):
        for t in range(2):
            for h in range(H):
                xe[s, pl.ds(t * H + h, 1), :] = row(even, depth_x(s, 1), h, depth_y(t, 0), 1, PAD)
                xe[s, pl.ds(2 * H + t * H + h, 1), :] = row(adm, depth_x(s, 2), h, depth_y(t, 0), OUT, PAD)
                for i, (dx, dy) in enumerate(near):
                    cs0[s, t, pl.ds(i * H + h, 1), :] = row(even, depth_x(s, dx), h, depth_y(t, dy), 1, PAD)
                for i, (dx, dy) in enumerate(near[:3]):
                    cs0[s, t, pl.ds((5 + i) * H + h, 1), :] = row(adm, depth_x(s, dx), h, depth_y(t, dy), OUT, PAD)

    beside_x = jnp.where(gx > 0, 1, 0) + jnp.where(gx < nx - 1, 1, 0)
    beside_y = jnp.where(gy > 0, 1, 0) + jnp.where(gy < ny - 1, 1, 0)
    pl.semaphore_wait(barrier, beside_x + beside_y + beside_x * beside_y)

    def to_x(s, src, dst):
        return send(src, dst, (xs[s], gy), there_x[s], there_x[1 - s])

    def to_y(t, src, dst):
        return send(src, dst, (gx, yside[t]), there_y[t], there_y[1 - t])

    def to_corner(s, t, src, dst):
        return send(src, dst, (xs[s], yside[t]), there_x[s] & there_y[t], there_x[1 - s] & there_y[1 - t])

    pending = [[] for _ in range(STEPS)]
    for s in range(2):
        pending[0].append(to_x(s, fs.at[0, s], fr.at[0, 1 - s]))
    for s in range(2):
        pending[0].append(to_x(s, xe.at[s], xer.at[1 - s]))
    for t in range(2):
        pending[0].append(to_y(t, ya.at[t], yar.at[1 - t]))
    for s, t in sides:
        pending[0].append(to_corner(s, t, cs0.at[s, t], cr0.at[1 - s, 1 - t]))
    for s in range(2):
        for d in range(2):
            pending[0].append(to_x(
                s, adm.at[depth_x(s, d) + OUT, :, pl.ds(PAD, Y), :], xa.at[1 - s, d]))
    loaded("o")
    loaded("n")

    every = list(range(T))
    for k in range(STEPS):
        now, then = (A, B) if k % 2 == 0 else (B, A)
        src, dst = (even, odd) if k % 2 == 0 else (odd, even)
        if k == STEPS - 1:
            loop(X, lambda x: alone(x, every, now, then, src, None), 4)
            break
        loop(2, lambda s: alone((X - 1) * s, every, now, then, src, dst, fs.at[k + 1, s]), 2)
        for s in range(2):
            pending[k + 1].append(to_x(s, fs.at[k + 1, s], fr.at[k + 1, 1 - s]))
        loop(X - 2, lambda i: alone(i + 1, every, now, then, src, dst), 7)
        for t in range(2):
            for h in range(H):
                ys[k + 1, t, h] = flat(dst)[line(dst, h, depth_y(t, 0), 1, PAD), :]
            pending[k + 1].append(to_y(t, ys.at[k + 1, t], yr.at[k + 1, 1 - t]))
        if k < 2:
            for s, t in sides:
                for h in range(H):
                    for i, (dx, dy) in enumerate(near[:3 if k == 0 else 1]):
                        cs1[k, s, t, pl.ds(i * H + h, 1), :] = row(dst, depth_x(s, dx), h, depth_y(t, dy), 1, PAD)
                pending[k + 1].append(to_corner(s, t, cs1.at[k, s, t], cr1.at[k, 1 - s, 1 - t]))

    def own_rows(k, t, h):
        return ya[t, pl.ds(h * X, X), :] if k == 0 else ys[k, t, h]

    def their_rows(k, t, h):
        return yar[t, pl.ds(h * X, X), :] if k == 0 else yr[k, t, h]

    def sources(k, then, dst):
        def plane(s, d, value):
            x = depth_x(s, d) + OUT

            def part(j):
                for h in range(H):
                    add = adm[x, h, rows(j, PAD), :] * value[h, rows(j), :]
                    then[x, h, rows(j, WIDE), :] = then[x, h, rows(j, WIDE), :] + add
                    dst[x, h, rows(j, WIDE), :] = dst[x, h, rows(j, WIDE), :] + al * add

            loop(T, part, T)

        def lines(y, h, value):
            add = flat_a[line(adm, h, y, OUT, PAD), :] * value
            for ref, scale in ((then, 1.0), (dst, al)):
                at = line(ref, h, y, OUT, WIDE)
                flat(ref)[at, :] = flat(ref)[at, :] + scale * add

        def cell(s, t, dx, dy, h, value):
            x, y = depth_x(s, dx) + OUT, depth_y(t, dy)
            add = adm[x, h, pl.ds(PAD + y, 1), :] * value
            at = pl.ds(WIDE + y, 1)
            then[x, h, at, :] = then[x, h, at, :] + add
            dst[x, h, at, :] = dst[x, h, at, :] + al * add

        for s in range(2):
            plane(s, 0, fr.at[k, s])
            plane(s, -1, fs.at[k, s])
        for t in range(2):
            for h in range(H):
                lines(depth_y(t, 0), h, their_rows(k, t, h))
                lines(depth_y(t, -1), h, own_rows(k, t, h))
        for s, t in sides:
            diagonal = cr0.at[s, t] if k == 0 else cr1.at[k - 1, s, t]
            for h in range(H):
                def at(i):
                    return diagonal[pl.ds(i * H + h, 1), :]

                cell(s, t, -1, 0, h, at(0))
                cell(s, t, 0, -1, h, at(0))
                if k < 2:
                    cell(s, t, -2, 0, h, at(1))
                    cell(s, t, 0, -2, h, at(2))
                    beside = fr[k, s, h, pl.ds(depth_y(t, 0), 1), :]
                    if k == 0:
                        beside = beside + yar[t, pl.ds(h * X + depth_x(s, 0), 1), :]
                    else:
                        beside = beside + yr[k, t, h, pl.ds(depth_x(s, 0), 1), :]
                    cell(s, t, -1, -1, h, beside)
                if k == 0:
                    cell(s, t, -3, 0, h, at(3))
                    cell(s, t, 0, -3, h, at(4))
                    cell(s, t, -2, -1, h, xer[s, pl.ds(t * H + h, 1), :])
                    cell(s, t, -1, -2, h, yar[t, pl.ds(3 * H * X + s * H + h, 1), :])

    for entry in pending[0]:
        arrived(entry)
    for s in range(2):
        for d in range(2):
            def place(j, s=s, d=d):
                for h in range(H):
                    adm[depth_x(s, -1 - d) + OUT, h, rows(j, PAD), :] = xa[s, d, h, rows(j), :]

            loop(T, place, T)
    for t in range(2):
        for h in range(H):
            for d in range(2):
                flat_a[line(adm, h, depth_y(t, -1 - d), OUT, PAD), :] = yar[t, pl.ds(((d + 1) * H + h) * X, X), :]
            for s in range(2):
                def put(dx, dy, value, s=s, t=t, h=h):
                    adm[depth_x(s, dx) + OUT, h, pl.ds(PAD + depth_y(t, dy), 1), :] = value

                put(0, -3, yar[t, pl.ds(3 * H * X + 2 * H + s * H + h, 1), :])
                put(-3, 0, xer[s, pl.ds(2 * H + t * H + h, 1), :])
                for i, (dx, dy) in enumerate(near[:3]):
                    put(-1 - dx, -1 - dy, cr0[s, t, pl.ds((5 + i) * H + h, 1), :])
    sources(0, dB, dD)

    around = [-1, 0, T - 1, T]
    full = list(range(-1, T + 1))
    frames = {
        1: [(-2, every), (-1, full), (0, full), (1, full)],
        2: [(-1, every), (0, full), (1, full), (2, full)],
        3: [(0, every), (1, every), (2, every), (3, every)],
    }
    for k in range(1, STEPS):
        now, then = (dA, dB) if k % 2 == 0 else (dB, dA)
        src, dst = (dE, dD) if k % 2 == 0 else (dD, dE)
        last_step = k == STEPS - 1

        def faces(s):
            for d, tiles in frames[k]:
                coupled(d + s * (X - 1 - 2 * d), tiles, now, then, src, None if last_step else dst)

        loop(2, faces)
        inner = k + 1
        middle = [0, T - 1] if last_step else around
        loop(X - 2 * inner, lambda i: coupled(i + inner, middle, now, then, src, None if last_step else dst), 2)
        for entry in pending[k]:
            arrived(entry)
        if not last_step:
            sources(k, then, dst)

    for s in range(2):
        x = depth_x(s, 0)

        def final(j, s=s, x=x):
            for h in range(H):
                A[x, h, rows(j), :] = A[x, h, rows(j), :] + (
                    adm[x + OUT, h, rows(j, PAD), :] * fr[STEPS - 1, s, h, rows(j), :])

        loop(T, final, T)
    for t in range(2):
        for h in range(H):
            at = line(A, h, depth_y(t, 0), 0, 0)
            flat(A)[at, :] = flat(A)[at, :] + (
                flat_a[line(adm, h, depth_y(t, 0), OUT, PAD), :] * yr[STEPS - 1, t, h])

    for group in pending:
        for entry in group:
            sent(entry)


def store_kernel(a, b, o, n, p_out, q_out, o_out, n_out, sems):
    copies = [
        pltpu.make_async_copy(src.at[:, h], dst.at[:, :, pl.ds(LANES * h, LANES)], sems.at[at, h])
        for at, (src, dst) in enumerate(((a, p_out), (b, q_out), (o, o_out), (n, n_out)))
        for h in range(2)
    ]
    for copy in copies:
        copy.start()
    for copy in copies:
        copy.wait()


def per_device(nx, ny, pressure, previous, oxygen_aux, nitrogen_aux, cell_class, wall_admittance, medium):
    X, Y, Z = pressure.shape
    H = Z // LANES
    split = (X, H, Y, LANES)
    padded = (X + 2, H, Y + 2 * PAD, LANES)
    wide = (X + 2 * OUT, H, Y + 2 * WIDE, LANES)
    hbm = pl.BlockSpec(memory_space=pl.ANY)
    vmem = pl.BlockSpec(memory_space=pltpu.VMEM)
    smem = pl.BlockSpec(memory_space=pltpu.SMEM)
    f32 = jnp.float32
    rows_y = 3 * H * X + 8
    state = pl.pallas_call(
        functools.partial(steps_kernel, nx, ny),
        out_shape=[pltpu.VMEM(split, f32)] * 4,
        in_specs=[hbm] * 5 + [smem] * 2,
        out_specs=[vmem] * 4,
        scratch_shapes=[
            pltpu.VMEM(split, jnp.int32),
            pltpu.VMEM((X + 2 * OUT, H, Y + 2 * PAD, LANES), f32),
            pltpu.VMEM(padded, f32),
            pltpu.VMEM(padded, f32),
            *[pltpu.VMEM(wide, f32)] * 6,
            pltpu.VMEM((STEPS, 2, H, Y, LANES), f32),
            pltpu.VMEM((STEPS, 2, H, X, LANES), f32),
            pltpu.VMEM((2, rows_y, LANES), f32),
            pltpu.VMEM((2, 8, LANES), f32),
            pltpu.VMEM((2, 2, 16, LANES), f32),
            pltpu.VMEM((2, 2, 2, 8, LANES), f32),
            pltpu.VMEM((STEPS, 2, H, Y, LANES), f32),
            pltpu.VMEM((2, 2, H, Y, LANES), f32),
            pltpu.VMEM((STEPS, 2, H, X, LANES), f32),
            pltpu.VMEM((2, rows_y, LANES), f32),
            pltpu.VMEM((2, 8, LANES), f32),
            pltpu.VMEM((2, 2, 16, LANES), f32),
            pltpu.VMEM((2, 2, 2, 8, LANES), f32),
            pltpu.SemaphoreType.DMA((5, 2)),
            pltpu.SemaphoreType.DMA((40,)),
            pltpu.SemaphoreType.DMA((40,)),
        ],
        compiler_params=pltpu.CompilerParams(
            collective_id=0, has_side_effects=True, vmem_limit_bytes=56 << 20),
    )(pressure, previous, oxygen_aux, nitrogen_aux, cell_class, wall_admittance, medium)
    out = pl.pallas_call(
        store_kernel,
        out_shape=[jax.ShapeDtypeStruct((X, Y, Z), f32)] * 4,
        in_specs=[vmem] * 4,
        out_specs=[hbm] * 4,
        scratch_shapes=[pltpu.SemaphoreType.DMA((4, 2))],
        compiler_params=pltpu.CompilerParams(vmem_limit_bytes=16 << 20),
    )(*state)
    return tuple(out)


def solution(mesh):
    field = P("gx", "gy", None)
    return jax.shard_map(
        functools.partial(per_device, mesh.shape["gx"], mesh.shape["gy"]),
        mesh=mesh,
        in_specs=(field,) * 5 + (P(), P()),
        out_specs=(field,) * 4,
        check_vma=False,
    )
```

```python
import functools

import jax
import jax.numpy as jnp
from jax import lax
from jax.experimental import pallas as pl
from jax.experimental.pallas import tpu as pltpu
from jax.sharding import PartitionSpec as P

STEPS = 4
NCLASS = 8
MESH = pl.DeviceIdType.MESH
LANES = 128
PAD = 8
WIDE = 16
OUT = 3


def steps_kernel(nx, ny, p_hbm, q_hbm, o_hbm, n_hbm, c_hbm, wall, medium, A, B, O, N,
                 cls, adm, even, odd, dA, dB, dO, dN, dE, dD,
                 x0, fs, ys, ya, cs, x0r, fr, yr, yar, cr,
                 load_sem, send_sem, recv_sem):
    X, H, Y, _ = A.shape
    T = Y // 8
    gx, gy = lax.axis_index("gx"), lax.axis_index("gy")
    xs = (lax.rem(gx + nx - 1, nx), lax.rem(gx + 1, nx))
    yside = (lax.rem(gy + ny - 1, ny), lax.rem(gy + 1, ny))
    there_x = (gx > 0, gx < nx - 1)
    there_y = (gy > 0, gy < ny - 1)
    sides = [(s, t) for s in range(2) for t in range(2)]

    barrier = pltpu.get_barrier_semaphore()
    others = [((xs[s], gy), there_x[s]) for s in range(2)]
    others += [((gx, yside[t]), there_y[t]) for t in range(2)]
    others += [((xs[s], yside[t]), there_x[s] & there_y[t]) for s, t in sides]
    for other, ok in others[::-1]:
        @pl.when(ok)
        def _():
            pl.semaphore_signal(barrier, inc=1, device_id=other, device_id_type=MESH)

    quarter = X // 4
    chunks = {"ends": ((0, quarter), (X - quarter, quarter)), "middle": ((quarter, X - 2 * quarter),)}
    groups = (("p", "q"), ("c",), ("o", "n"))
    source = {"p": (p_hbm, A), "q": (q_hbm, B), "c": (c_hbm, cls), "o": (o_hbm, O), "n": (n_hbm, N)}
    order = [(names, part) for part in ("ends", "middle") for names in groups]
    for at, (names, part) in enumerate(order):
        for name in names:
            src, dst = source[name]
            for x, count in chunks[part]:
                for h in range(H):
                    pltpu.make_async_copy(
                        src.at[pl.ds(x, count), :, pl.ds(LANES * h, LANES)],
                        dst.at[pl.ds(x, count), h], load_sem.at[at]).start()

    def loaded(names, part):
        planes = len(names) * sum(count for _, count in chunks[part])
        whole = A.at[pl.ds(0, planes)]
        pltpu.make_async_copy(whole, whole, load_sem.at[order.index((names, part))]).wait()

    m0, m1, m2, m3 = medium[0], medium[1], medium[2], medium[3]
    c = 0.05 * medium[4]
    al = 0.33 + c

    lane = lax.broadcasted_iota(jnp.int32, (8, LANES), 1)
    first, last = lane == 0, lane == LANES - 1
    zero = jnp.zeros((8, LANES), jnp.float32)

    def loop(count, body, unroll=1):
        lax.fori_loop(0, count, lambda i, carry: (body(i), carry)[1], 0, unroll=unroll)

    def rows(j, pad=0, by=0):
        return pl.ds(pad + 8 * j + by, 8)

    def depth_x(s, d):
        return d if s == 0 else X - 1 - d

    def depth_y(t, d):
        return d if t == 0 else Y - 1 - d

    def advance(x, j, now, then, oxy, nit, xo, pad, src, wx, wpad, fresh=False, across=None):
        w = [src[x + wx, h, rows(j, wpad), :] for h in range(H)]
        down = [pltpu.roll(v, 1, 1) for v in w]
        up = [pltpu.roll(v, LANES - 1, 1) for v in w]
        below = [jnp.where(first, 0.0, down[0]), jnp.where(first, down[0], down[1])]
        above = [jnp.where(last, up[1], up[0]), jnp.where(last, 0.0, up[1])]
        result = []
        for h in range(H):
            at = (x + xo, h, rows(j, pad), slice(None))
            p = now[at]
            total = src[x + wx - 1, h, rows(j, wpad), :] + src[x + wx + 1, h, rows(j, wpad), :]
            total = total + (src[x + wx, h, rows(j, wpad, -1), :] + src[x + wx, h, rows(j, wpad, 1), :])
            total = total + (below[h] + above[h])
            if across is not None and 0 <= j < T:
                total = total + across(h, 8 * j, 8)
            a = adm[x + OUT, h, rows(j, PAD), :]
            if fresh:
                o, n = m1 * p, m3 * p
                new = a * ((total - 6.0 * w[h]) + (2.0 * p - (o + n)))
            else:
                q = then[at]
                d = p - q
                o = m0 * oxy[at] + m1 * d
                n = m2 * nit[at] + m3 * d
                new = q + a * ((total - 6.0 * w[h]) + (2.0 * d - (o + n)))
            result.append((h, at, p, new, o, n))
        return result

    def alone(x, tiles, now, then, src, dst, keep=None):
        for j0 in range(0, len(tiles), 2):
            done = [(j, r) for j in tiles[j0:j0 + 2] for r in advance(x, j, now, then, O, N, 0, 0, src, 1, PAD)]
            for j, (h, at, p, new, o, n) in done:
                then[at] = new
                O[at] = o
                N[at] = n
                if dst is not None:
                    v = al * new - c * p
                    dst[x + 1, h, rows(j, PAD), :] = v
                    if keep is not None:
                        keep[h, rows(j), :] = v

    def coupled(x, tiles, now, then, src, dst, fresh, across=None):
        for j0 in range(0, len(tiles), 2):
            done = [(j, r) for j in tiles[j0:j0 + 2]
                    for r in advance(x, j, now, then, dO, dN, OUT, WIDE, src, OUT, WIDE, fresh, across)]
            for j, (h, at, p, new, o, n) in done:
                if dst is not None:
                    then[at] = new
                    dO[at] = o
                    dN[at] = n
                    dst[at] = al * new - c * p
                else:
                    to = (x, h, rows(j), slice(None))
                    A[to] = A[to] + new
                    B[to] = B[to] + p
                    O[to] = O[to] + o
                    N[to] = N[to] + n

    def flat(ref):
        planes, halves, height, _ = ref.shape
        return ref.reshape(planes * halves * height, LANES)

    def line(ref, h, y, xo, pad):
        height = ref.shape[2]
        return pl.ds((xo * H + h) * height + pad + y, X, stride=H * height)

    messages = iter(range(recv_sem.shape[0]))
    in_flight = [[0, ok] for _, ok in others]

    def send(group, src, dst, device, ok, back, now):
        at = next(messages)
        in_flight[group][0] += src.size // LANES

        def describe():
            return pltpu.make_async_remote_copy(
                src_ref=src, dst_ref=dst, send_sem=send_sem.at[group], recv_sem=recv_sem.at[at],
                device_id=device, device_id_type=MESH)

        def start(when):
            @pl.when(ok & when)
            def _():
                describe().start()

        if now is None:
            held.append(start)
        else:
            start(now)
        return describe, back

    def arrived(entry):
        @pl.when(entry[1])
        def _():
            entry[0]().wait_recv()

    def clear(x):
        for ref in (dE, dD, dB):
            for h in range(H):
                for j in range(-2, T + 2):
                    ref[x, h, rows(j, WIDE), :] = zero
        for h in range(H):
            adm[x, h, rows(-1, PAD), :] = zero
            adm[x, h, rows(T, PAD), :] = zero

    def clear_next(i):
        for d in (2, 3):
            for ref in (dA, dO, dN):
                for h in range(H):
                    for j in range(T):
                        ref[d + i * (X - 1 - 2 * d) + OUT, h, rows(j, WIDE), :] = zero

    def clear_own(x):
        for h in range(H):
            for ref in (even, odd):
                ref[x, h, rows(-1, PAD), :] = zero
                ref[x, h, rows(T, PAD), :] = zero

    def clear_faces(j):
        for h in range(H):
            for ref in (even, odd):
                for x in (0, X + 1):
                    ref[x, h, rows(j, PAD), :] = zero
            for x in (0, X + 2 * OUT - 1):
                adm[x, h, rows(j, PAD), :] = zero

    loop(X + 2 * OUT, clear)
    loop(2, clear_next)
    loop(X + 2, clear_own)
    loop(T, clear_faces)
    blank = jnp.zeros((X, LANES), jnp.float32)
    for s in range(2):
        @pl.when(jnp.logical_not(there_x[s]))
        def _():
            def none(j):
                for h in range(H):
                    for k in range(STEPS - 1):
                        fr[k, s, h, rows(j), :] = zero

            def none_first(i):
                x0r[s, pl.ds(8 * i, 8), :] = zero

            loop(T, none)
            loop(x0.shape[1] // 8, none_first, 5)

        @pl.when(jnp.logical_not(there_y[s]))
        def _():
            for h in range(H):
                for k in range(STEPS - 1):
                    yr[k, s, h] = blank
                for f in range(3):
                    yar[s, pl.ds((f * H + h) * X, X), :] = blank
            yar[s, pl.ds(3 * H * X, 8), :] = zero

        for t in range(2):
            @pl.when(jnp.logical_not(there_x[s] & there_y[t]))
            def _():
                for i in range(3):
                    cr[s, t, pl.ds(8 * i, 8), :] = zero

    def first_w(x, keep=None):
        for j in range(T):
            for h in range(H):
                v = al * A[x, h, rows(j), :] - c * B[x, h, rows(j), :]
                even[x + 1, h, rows(j, PAD), :] = v
                if keep is not None:
                    x0[keep, rows(j, h * Y), :] = v

    extra = 2 * H * Y
    table = [1.0 / (1.0 + 0.5 * jnp.full((8, LANES), wall[k], jnp.float32)) for k in range(1, NCLASS)]

    def admit(x, keep=None, field=0):
        for j in range(T):
            for h in range(H):
                kind = cls[x, h, rows(j), :]
                a = jnp.ones((8, LANES), jnp.float32)
                for k in range(1, NCLASS):
                    a = jnp.where(kind == k, table[k - 1], a)
                adm[x + OUT, h, rows(j, PAD), :] = a
                if keep is not None:
                    x0[keep, rows(j, (field * H + h) * Y + (16 if field == 2 else 0)), :] = a

    def row(ref, x, h, y, xo, pad):
        return ref[x + xo, h, pl.ds(pad + y, 1), :]

    def to_x(s, src, dst, now):
        return send(s, src, dst, (xs[s], gy), there_x[s], there_x[1 - s], now)

    def to_y(t, src, dst, now):
        return send(2 + t, src, dst, (gx, yside[t]), there_y[t], there_y[1 - t], now)

    def to_corner(s, t, src, dst, now):
        return send(4 + 2 * s + t, src, dst, (xs[s], yside[t]), there_x[s] & there_y[t],
                    there_x[1 - s] & there_y[1 - t], now)

    ring = max(nx // 4, 1)
    early = (lax.rem(gx, ring) == 0) & (gx > 0)
    late = jnp.logical_not(early)
    held = []

    beside_x = jnp.where(gx > 0, 1, 0) + jnp.where(gx < nx - 1, 1, 0)
    beside_y = jnp.where(gy > 0, 1, 0) + jnp.where(gy < ny - 1, 1, 0)

    def greet(who):
        @pl.when(who)
        def _():
            pl.semaphore_wait(barrier, beside_x + beside_y + beside_x * beside_y)

    every = list(range(T))
    states = [(A, B, even, odd), (B, A, odd, even), (A, B, even, odd), (B, A, odd, None)]
    near = ((0, 0), (1, 0), (0, 1), (2, 0), (0, 2))

    def end(s, d):
        return d + s * (X - 1 - 2 * d)

    def lines_out(first_line, ref, xo, cells):
        for s, t in sides:
            for h in range(H):
                for i, (dx, dy) in enumerate(cells):
                    cs[s, t, pl.ds((first_line + i) * H + h, 1), :] = row(
                        ref, depth_x(s, dx), h, depth_y(t, dy), xo, PAD)

    def begin(s):
        first_w(end(s, 0), s)
        for d in range(1, quarter):
            first_w(end(s, d))

    def admit_ends(s):
        for d in range(quarter):
            admit(end(s, d), s if d < 2 else None, d + 1)

    loaded(("p", "q"), "ends")
    loop(2, begin)
    loaded(("c",), "ends")
    loop(2, admit_ends)
    lines_out(0, even, 1, near)
    lines_out(5, adm, OUT, near[:3])
    for s, t in sides:
        for h in range(H):
            x0[s, pl.ds(extra + t * H + h, 1), :] = row(even, depth_x(s, 1), h, depth_y(t, 0), 1, PAD)
            for i, d in enumerate((2, 1)):
                x0[s, pl.ds(extra + 2 * H * (i + 1) + t * H + h, 1), :] = row(
                    adm, depth_x(s, d), h, depth_y(t, 0), OUT, PAD)
    pending = [[] for _ in range(STEPS)]
    starts = []

    def both(make):
        held.clear()
        entry = make(None)
        held[0](late)
        starts.append(held[0])
        return entry

    greet(late)
    for s, t in sides:
        pending[0].append(both(lambda now: to_corner(
            s, t, cs.at[s, t, pl.ds(0, 16)], cr.at[1 - s, 1 - t, pl.ds(0, 16)], now)))
    second = []
    for part, rows_sent, entries in ((0, extra + 16, pending[0]), (extra + 16, H * Y, second)):
        for s in range(2):
            entries.append(both(lambda now: to_x(
                s, x0.at[s, pl.ds(part, rows_sent)], x0r.at[1 - s, pl.ds(part, rows_sent)], now)))
    loaded(("o", "n"), "ends")
    for k in range(3):
        def narrow(s, k=k):
            for d in range(3 - k):
                alone(end(s, d), every, *states[k], fs.at[k, s] if d == 0 else None)

        loop(2, narrow)
        if k < 2:
            lines_out(8 + 3 * k, states[k][3], 1, near[:3 if k == 0 else 1])
        if k == 1:
            for s, t in sides:
                pending[1].append(both(lambda now: to_corner(
                    s, t, cs.at[s, t, pl.ds(16, 8)], cr.at[1 - s, 1 - t, pl.ds(16, 8)], now)))
        for layer in ((), (0, 1), (2,))[k]:
            for s in range(2):
                pending[layer + 1].append(both(lambda now: to_x(s, fs.at[layer, s], fr.at[layer, 1 - s], now)))

    loaded(("p", "q"), "middle")
    loop(X - 2 * quarter, lambda i: first_w(i + quarter), 4)
    loaded(("c",), "middle")
    loop(X - 2 * quarter, lambda i: admit(i + quarter), 4)
    flat_a = flat(adm)
    for t in range(2):
        for h in range(H):
            for s in range(2):
                ya[t, pl.ds(3 * H * X + s * H + h, 1), :] = cs[s, t, pl.ds(2 * H + h, 1), :]
                ya[t, pl.ds(3 * H * X + 2 * H + s * H + h, 1), :] = row(
                    adm, depth_x(s, 0), h, depth_y(t, 2), OUT, PAD)
            ya[t, pl.ds(h * X, X), :] = flat(even)[line(even, h, depth_y(t, 0), 1, PAD), :]
            for d in range(2):
                ya[t, pl.ds(((d + 1) * H + h) * X, X), :] = flat_a[line(adm, h, depth_y(t, d), OUT, PAD), :]
        for s in range(2):
            for h in range(H):
                for d in range(2):
                    ya[t, pl.ds(h * X + depth_x(s, d), 1), :] = cs[s, t, pl.ds(d * H + h, 1), :]
        pending[0].append(both(lambda now: to_y(t, ya.at[t], yar.at[1 - t], now)))
    loaded(("o", "n"), "middle")
    for k in range(STEPS):
        done = 3 - k
        if k == STEPS - 1:
            loop(X, lambda x: alone(x, every, *states[k]), 4)
            break
        loop(X - 2 * done, lambda i: alone(i + done, every, *states[k]), (5, 6, 7)[k])
        for t in range(2):
            for h in range(H):
                dst = states[k][3]
                ys[k, t, h] = flat(dst)[line(dst, h, depth_y(t, 0), 1, PAD), :]
                for s in range(2):
                    if k < 2:
                        for d in range(2 - k):
                            ys[k, t, h, pl.ds(depth_x(s, d), 1), :] = (
                                fs[k, s, h, pl.ds(depth_y(t, 0), 1), :] if d == 0
                                else cs[s, t, pl.ds((8 + d) * H + h, 1), :])
            if k < 2:
                pending[k + 1].append(both(lambda now: to_y(t, ys.at[k, t], yr.at[k, 1 - t], now)))
            else:
                pending[k + 1].append(to_y(t, ys.at[k, t], yr.at[k, 1 - t], late | early))
        if k == 1:
            greet(early)
            for start in starts:
                start(early)

    def own_rows(k, t, h):
        return ya[t, pl.ds(h * X, X), :] if k == 0 else ys[k - 1, t, h]

    def their_rows(k, t, h):
        return yar[t, pl.ds(h * X, X), :] if k == 0 else yr[k - 1, t, h]

    def own_plane(k, s, h, at, size):
        return x0[s, pl.ds(h * Y + at, size), :] if k == 0 else fs[k - 1, s, h, pl.ds(at, size), :]

    def their_plane(k, s, h, at, size):
        return x0r[s, pl.ds(h * Y + at, size), :] if k == 0 else fr[k - 1, s, h, pl.ds(at, size), :]

    def sources(k, then, dst):
        def plane(s, d, value):
            x = depth_x(s, d) + OUT

            def part(j):
                for h in range(H):
                    add = adm[x, h, rows(j, PAD), :] * value(k, s, h, 8 * j, 8)
                    then[x, h, rows(j, WIDE), :] = then[x, h, rows(j, WIDE), :] + add
                    dst[x, h, rows(j, WIDE), :] = dst[x, h, rows(j, WIDE), :] + al * add

            loop(T, part, T)

        def lines(y, h, value):
            add = flat_a[line(adm, h, y, OUT, PAD), :] * value
            for ref, scale in ((then, 1.0), (dst, al)):
                at = line(ref, h, y, OUT, WIDE)
                flat(ref)[at, :] = flat(ref)[at, :] + scale * add

        def cell(s, t, dx, dy, h, value):
            x, y = depth_x(s, dx) + OUT, depth_y(t, dy)
            add = adm[x, h, pl.ds(PAD + y, 1), :] * value
            at = pl.ds(WIDE + y, 1)
            then[x, h, at, :] = then[x, h, at, :] + add
            dst[x, h, at, :] = dst[x, h, at, :] + al * add

        if k == 0:
            for s in range(2):
                plane(s, 0, their_plane)
                plane(s, -1, own_plane)
        for t in range(2):
            for h in range(H):
                lines(depth_y(t, 0), h, their_rows(k, t, h))
                lines(depth_y(t, -1), h, own_rows(k, t, h))
        for s, t in sides:
            base = (0, 8, 11)[k]
            for h in range(H):
                def at(i):
                    return cr[s, t, pl.ds((base + i) * H + h, 1), :]

                cell(s, t, -1, 0, h, at(0))
                cell(s, t, 0, -1, h, at(0))
                if k < 2:
                    cell(s, t, -2, 0, h, at(1))
                    cell(s, t, 0, -2, h, at(2))
                    beside = their_plane(k, s, h, depth_y(t, 0), 1)
                    if k == 0:
                        beside = beside + yar[t, pl.ds(h * X + depth_x(s, 0), 1), :]
                    else:
                        beside = beside + yr[k - 1, t, h, pl.ds(depth_x(s, 0), 1), :]
                    cell(s, t, -1, -1, h, beside)
                if k == 0:
                    cell(s, t, -3, 0, h, at(3))
                    cell(s, t, 0, -3, h, at(4))
                    cell(s, t, -2, -1, h, x0r[s, pl.ds(extra + t * H + h, 1), :])
                    cell(s, t, -1, -2, h, yar[t, pl.ds(3 * H * X + s * H + h, 1), :])

    for entry in pending[0]:
        arrived(entry)
    def place(d):
        for s in range(2):
            def part(j, s=s):
                for h in range(H):
                    adm[depth_x(s, -1 - d) + OUT, h, rows(j, PAD), :] = x0r[
                        s, rows(j, ((d + 1) * H + h) * Y + 16 * d), :]

            loop(T, part, T)

    place(0)
    for t in range(2):
        for h in range(H):
            for d in range(2):
                flat_a[line(adm, h, depth_y(t, -1 - d), OUT, PAD), :] = yar[t, pl.ds(((d + 1) * H + h) * X, X), :]
            for s in range(2):
                def put(dx, dy, value, s=s, t=t, h=h):
                    adm[depth_x(s, dx) + OUT, h, pl.ds(PAD + depth_y(t, dy), 1), :] = value

                put(0, -3, yar[t, pl.ds(3 * H * X + 2 * H + s * H + h, 1), :])
                for i, d in enumerate((-3, -2)):
                    put(d, 0, x0r[s, pl.ds(extra + 2 * H * (i + 1) + t * H + h, 1), :])
                for i, (dx, dy) in enumerate(near[:3]):
                    put(-1 - dx, -1 - dy, cr[s, t, pl.ds((5 + i) * H + h, 1), :])
    sources(0, dB, dD)

    around = [-1, 0, T - 1, T]
    full = list(range(-1, T + 1))
    frames = {
        1: [(-2, every), (-1, full), (0, full), (1, full)],
        2: [(-1, every), (0, full), (1, full), (2, full)],
        3: [(0, every), (1, every), (2, every), (3, every)],
    }
    for k in range(1, STEPS):
        now, then = (dA, dB) if k % 2 == 0 else (dB, dA)
        src, dst = (dE, dD) if k % 2 == 0 else (dD, dE)
        last_step = k == STEPS - 1

        step = (now, then, src, None if last_step else dst, k == 1)
        inner = k + 1
        middle = [0, T - 1] if last_step else around
        loop(X - 2 * inner, lambda i: coupled(i + inner, middle, *step), (0, 6, 5, 8)[k])

        def faces(s):
            for d, tiles in frames[k]:
                if d not in (0, -1):
                    coupled(end(s, d), tiles, *step)

        def touching(s):
            for d, tiles in frames[k]:
                if d == 0:
                    coupled(end(s, d), tiles, *step, lambda h, at, size: their_plane(k, s, h, at, size))
                if d == -1:
                    coupled(end(s, d), tiles, *step, lambda h, at, size: own_plane(k, s, h, at, size))

        if k == 1:
            for entry in second:
                arrived(entry)
            place(1)
        loop(2, faces)
        for entry in pending[k]:
            arrived(entry)
        loop(2, touching)
        if not last_step:
            sources(k, then, dst)

    for t in range(2):
        for h in range(H):
            at = line(A, h, depth_y(t, 0), 0, 0)
            flat(A)[at, :] = flat(A)[at, :] + (
                flat_a[line(adm, h, depth_y(t, 0), OUT, PAD), :] * yr[STEPS - 2, t, h])

    for at, (size, ok) in enumerate(in_flight):
        @pl.when(ok)
        def _():
            whole = flat(dE).at[pl.ds(0, size)]
            pltpu.make_async_copy(whole, whole, send_sem.at[at]).wait()


def store_kernel(a, b, o, n, p_out, q_out, o_out, n_out, sems):
    pairs = ((a, p_out), (b, q_out), (o, o_out), (n, n_out))
    for at, (src, dst) in enumerate(pairs):
        for h in range(2):
            pltpu.make_async_copy(src.at[:, h], dst.at[:, :, pl.ds(LANES * h, LANES)], sems.at[at]).start()
    for at, (src, dst) in enumerate(pairs):
        pltpu.make_async_copy(src, src, sems.at[at]).wait()


def per_device(nx, ny, pressure, previous, oxygen_aux, nitrogen_aux, cell_class, wall_admittance, medium):
    X, Y, Z = pressure.shape
    H = Z // LANES
    split = (X, H, Y, LANES)
    padded = (X + 2, H, Y + 2 * PAD, LANES)
    wide = (X + 2 * OUT, H, Y + 2 * WIDE, LANES)
    hbm = pl.BlockSpec(memory_space=pl.ANY)
    vmem = pl.BlockSpec(memory_space=pltpu.VMEM)
    smem = pl.BlockSpec(memory_space=pltpu.SMEM)
    f32 = jnp.float32
    rows_y = 3 * H * X + 8
    state = pl.pallas_call(
        functools.partial(steps_kernel, nx, ny),
        out_shape=[pltpu.VMEM(split, f32)] * 4,
        in_specs=[hbm] * 5 + [smem] * 2,
        out_specs=[vmem] * 4,
        scratch_shapes=[
            pltpu.VMEM(split, jnp.int32),
            pltpu.VMEM((X + 2 * OUT, H, Y + 2 * PAD, LANES), f32),
            pltpu.VMEM(padded, f32),
            pltpu.VMEM(padded, f32),
            *[pltpu.VMEM(wide, f32)] * 6,
            pltpu.VMEM((2, 3 * H * Y + 16, LANES), f32),
            pltpu.VMEM((STEPS - 1, 2, H, Y, LANES), f32),
            pltpu.VMEM((STEPS - 1, 2, H, X, LANES), f32),
            pltpu.VMEM((2, rows_y, LANES), f32),
            pltpu.VMEM((2, 2, 24, LANES), f32),
            pltpu.VMEM((2, 3 * H * Y + 16, LANES), f32),
            pltpu.VMEM((STEPS - 1, 2, H, Y, LANES), f32),
            pltpu.VMEM((STEPS - 1, 2, H, X, LANES), f32),
            pltpu.VMEM((2, rows_y, LANES), f32),
            pltpu.VMEM((2, 2, 24, LANES), f32),
            pltpu.SemaphoreType.DMA((6,)),
            pltpu.SemaphoreType.DMA((8,)),
            pltpu.SemaphoreType.DMA((26,)),
        ],
        compiler_params=pltpu.CompilerParams(
            collective_id=0, has_side_effects=True, vmem_limit_bytes=56 << 20),
    )(pressure, previous, oxygen_aux, nitrogen_aux, cell_class, wall_admittance, medium)
    out = pl.pallas_call(
        store_kernel,
        out_shape=[jax.ShapeDtypeStruct((X, Y, Z), f32)] * 4,
        in_specs=[vmem] * 4,
        out_specs=[hbm] * 4,
        scratch_shapes=[pltpu.SemaphoreType.DMA((4,))],
        compiler_params=pltpu.CompilerParams(vmem_limit_bytes=16 << 20),
    )(*state)
    return tuple(out)


def solution(mesh):
    field = P("gx", "gy", None)
    return jax.shard_map(
        functools.partial(per_device, mesh.shape["gx"], mesh.shape["gy"]),
        mesh=mesh,
        in_specs=(field,) * 5 + (P(), P()),
        out_specs=(field,) * 4,
        check_vma=False,
    )
```

```python
import functools

import jax
import jax.numpy as jnp
from jax import lax
from jax.experimental import pallas as pl
from jax.experimental.pallas import tpu as pltpu
from jax.sharding import PartitionSpec as P

STEPS = 4
NCLASS = 8
MESH = pl.DeviceIdType.MESH
LANES = 128
PAD = 8
WIDE = 16
OUT = 3


def steps_kernel(nx, ny, p_hbm, q_hbm, o_hbm, n_hbm, c_hbm, wall, medium, A, B, O, N,
                 cls, adm, even, odd, dA, dB, dO, dN, dE, dD,
                 x0, fs, ys, ya, cs, x0r, fr, yr, yar, cr,
                 load_sem, send_sem, recv_sem):
    X, H, Y, _ = A.shape
    T = Y // 8
    gx, gy = lax.axis_index("gx"), lax.axis_index("gy")
    xs = (lax.rem(gx + nx - 1, nx), lax.rem(gx + 1, nx))
    yside = (lax.rem(gy + ny - 1, ny), lax.rem(gy + 1, ny))
    there_x = (gx > 0, gx < nx - 1)
    there_y = (gy > 0, gy < ny - 1)
    sides = [(s, t) for s in range(2) for t in range(2)]

    barrier = pltpu.get_barrier_semaphore()
    others = [((xs[s], gy), there_x[s]) for s in range(2)]
    others += [((gx, yside[t]), there_y[t]) for t in range(2)]
    others += [((xs[s], yside[t]), there_x[s] & there_y[t]) for s, t in sides]
    for other, ok in others[::-1]:
        @pl.when(ok)
        def _():
            pl.semaphore_signal(barrier, inc=1, device_id=other, device_id_type=MESH)

    quarter = X // 4
    chunks = {"ends": ((0, quarter), (X - quarter, quarter)), "middle": ((quarter, X - 2 * quarter),)}
    groups = (("p", "q"), ("c",), ("o", "n"))
    source = {"p": (p_hbm, A), "q": (q_hbm, B), "c": (c_hbm, cls), "o": (o_hbm, O), "n": (n_hbm, N)}
    order = [(names, part) for part in ("ends", "middle") for names in groups]
    for at, (names, part) in enumerate(order):
        for name in names:
            src, dst = source[name]
            for x, count in chunks[part]:
                for h in range(H):
                    pltpu.make_async_copy(
                        src.at[pl.ds(x, count), :, pl.ds(LANES * h, LANES)],
                        dst.at[pl.ds(x, count), h], load_sem.at[at]).start()

    def loaded(names, part):
        planes = len(names) * sum(count for _, count in chunks[part])
        whole = A.at[pl.ds(0, planes)]
        pltpu.make_async_copy(whole, whole, load_sem.at[order.index((names, part))]).wait()

    m0, m1, m2, m3 = medium[0], medium[1], medium[2], medium[3]
    c = 0.05 * medium[4]
    al = 0.33 + c

    lane = lax.broadcasted_iota(jnp.int32, (8, LANES), 1)
    first, last = lane == 0, lane == LANES - 1
    zero = jnp.zeros((8, LANES), jnp.float32)

    def loop(count, body, unroll=1):
        lax.fori_loop(0, count, lambda i, carry: (body(i), carry)[1], 0, unroll=unroll)

    def rows(j, pad=0, by=0):
        return pl.ds(pad + 8 * j + by, 8)

    def depth_x(s, d):
        return d if s == 0 else X - 1 - d

    def depth_y(t, d):
        return d if t == 0 else Y - 1 - d

    def advance(x, j, now, then, oxy, nit, xo, pad, src, wx, wpad, fresh=False, across=None):
        w = [src[x + wx, h, rows(j, wpad), :] for h in range(H)]
        down = [pltpu.roll(v, 1, 1) for v in w]
        up = [pltpu.roll(v, LANES - 1, 1) for v in w]
        below = [jnp.where(first, 0.0, down[0]), jnp.where(first, down[0], down[1])]
        above = [jnp.where(last, up[1], up[0]), jnp.where(last, 0.0, up[1])]
        result = []
        for h in range(H):
            at = (x + xo, h, rows(j, pad), slice(None))
            p = now[at]
            total = src[x + wx - 1, h, rows(j, wpad), :] + src[x + wx + 1, h, rows(j, wpad), :]
            total = total + (src[x + wx, h, rows(j, wpad, -1), :] + src[x + wx, h, rows(j, wpad, 1), :])
            total = total + (below[h] + above[h])
            beyond = across(h, j) if across is not None else None
            if beyond is not None:
                total = total + beyond
            a = adm[x + OUT, h, rows(j, PAD), :]
            if fresh:
                o, n = m1 * p, m3 * p
                new = a * ((total - 6.0 * w[h]) + (2.0 * p - (o + n)))
            else:
                q = then[at]
                d = p - q
                o = m0 * oxy[at] + m1 * d
                n = m2 * nit[at] + m3 * d
                new = q + a * ((total - 6.0 * w[h]) + (2.0 * d - (o + n)))
            result.append((h, at, p, new, o, n))
        return result

    def alone(x, tiles, now, then, src, dst, keep=None):
        for j0 in range(0, len(tiles), 2):
            done = [(j, r) for j in tiles[j0:j0 + 2] for r in advance(x, j, now, then, O, N, 0, 0, src, 1, PAD)]
            for j, (h, at, p, new, o, n) in done:
                then[at] = new
                O[at] = o
                N[at] = n
                if dst is not None:
                    v = al * new - c * p
                    dst[x + 1, h, rows(j, PAD), :] = v
                    if keep is not None:
                        keep[h, rows(j), :] = v

    def coupled(x, tiles, now, then, src, dst, fresh, across=None):
        for j0 in range(0, len(tiles), 2):
            done = [(j, r) for j in tiles[j0:j0 + 2]
                    for r in advance(x, j, now, then, dO, dN, OUT, WIDE, src, OUT, WIDE, fresh, across)]
            for j, (h, at, p, new, o, n) in done:
                if dst is not None:
                    then[at] = new
                    dO[at] = o
                    dN[at] = n
                    dst[at] = al * new - c * p
                else:
                    to = (x, h, rows(j), slice(None))
                    A[to] = A[to] + new
                    B[to] = B[to] + p
                    O[to] = O[to] + o
                    N[to] = N[to] + n

    def flat(ref):
        planes, halves, height, _ = ref.shape
        return ref.reshape(planes * halves * height, LANES)

    def line(ref, h, y, xo, pad):
        height = ref.shape[2]
        return pl.ds((xo * H + h) * height + pad + y, X, stride=H * height)

    messages = iter(range(recv_sem.shape[0]))
    in_flight = [[0, ok] for _, ok in others]

    def send(group, src, dst, device, ok, back, now):
        at = next(messages)
        in_flight[group][0] += src.size // LANES

        def describe():
            return pltpu.make_async_remote_copy(
                src_ref=src, dst_ref=dst, send_sem=send_sem.at[group], recv_sem=recv_sem.at[at],
                device_id=device, device_id_type=MESH)

        def start(when):
            @pl.when(ok & when)
            def _():
                describe().start()

        if now is None:
            held.append(start)
        else:
            start(now)
        return describe, back

    def arrived(entry):
        @pl.when(entry[1])
        def _():
            entry[0]().wait_recv()

    def clear(x):
        for ref in (dE, dD, dB):
            for h in range(H):
                for j in range(-2, T + 2):
                    ref[x, h, rows(j, WIDE), :] = zero
        for h in range(H):
            adm[x, h, rows(-1, PAD), :] = zero
            adm[x, h, rows(T, PAD), :] = zero

    def clear_next(i):
        for d in (2, 3):
            for ref in (dA, dO, dN):
                for h in range(H):
                    for j in range(T):
                        ref[d + i * (X - 1 - 2 * d) + OUT, h, rows(j, WIDE), :] = zero

    def clear_own(x):
        for h in range(H):
            for ref in (even, odd):
                ref[x, h, rows(-1, PAD), :] = zero
                ref[x, h, rows(T, PAD), :] = zero

    def clear_faces(j):
        for h in range(H):
            for ref in (even, odd):
                for x in (0, X + 1):
                    ref[x, h, rows(j, PAD), :] = zero
            for x in (0, X + 2 * OUT - 1):
                adm[x, h, rows(j, PAD), :] = zero

    loop(X + 2 * OUT, clear)
    loop(2, clear_next)
    loop(X + 2, clear_own)
    loop(T, clear_faces)
    blank = jnp.zeros((X, LANES), jnp.float32)
    for s in range(2):
        @pl.when(jnp.logical_not(there_x[s]))
        def _():
            def none(j):
                for h in range(H):
                    for k in range(STEPS - 1):
                        fr[k, s, h, rows(j), :] = zero

            def none_first(i):
                x0r[s, pl.ds(8 * i, 8), :] = zero

            loop(T, none)
            loop(x0.shape[1] // 8, none_first, 5)

        @pl.when(jnp.logical_not(there_y[s]))
        def _():
            for h in range(H):
                for k in range(STEPS - 1):
                    yr[k, s, h] = blank
                for f in range(3):
                    yar[s, pl.ds((f * H + h) * X, X), :] = blank
            yar[s, pl.ds(3 * H * X, 8), :] = zero

        for t in range(2):
            @pl.when(jnp.logical_not(there_x[s] & there_y[t]))
            def _():
                for i in range(3):
                    cr[s, t, pl.ds(8 * i, 8), :] = zero

    def first_w(x, keep=None):
        for j in range(T):
            for h in range(H):
                v = al * A[x, h, rows(j), :] - c * B[x, h, rows(j), :]
                even[x + 1, h, rows(j, PAD), :] = v
                if keep is not None:
                    x0[keep, rows(j, h * Y), :] = v

    extra = 2 * H * Y
    table = [1.0 / (1.0 + 0.5 * jnp.full((8, LANES), wall[k], jnp.float32)) for k in range(1, NCLASS)]

    def admit(x, keep=None, field=0):
        for j in range(T):
            for h in range(H):
                kind = cls[x, h, rows(j), :]
                a = jnp.ones((8, LANES), jnp.float32)
                for k in range(1, NCLASS):
                    a = jnp.where(kind == k, table[k - 1], a)
                adm[x + OUT, h, rows(j, PAD), :] = a
                if keep is not None:
                    x0[keep, rows(j, (field * H + h) * Y + (16 if field == 2 else 0)), :] = a

    def row(ref, x, h, y, xo, pad):
        return ref[x + xo, h, pl.ds(pad + y, 1), :]

    def to_x(s, src, dst, now):
        return send(s, src, dst, (xs[s], gy), there_x[s], there_x[1 - s], now)

    def to_y(t, src, dst, now):
        return send(2 + t, src, dst, (gx, yside[t]), there_y[t], there_y[1 - t], now)

    def to_corner(s, t, src, dst, now):
        return send(4 + 2 * s + t, src, dst, (xs[s], yside[t]), there_x[s] & there_y[t],
                    there_x[1 - s] & there_y[1 - t], now)

    ring = max(nx // 4, 1)
    early = (lax.rem(gx, ring) == 0) & (gx > 0)
    late = jnp.logical_not(early)
    held = []

    beside_x = jnp.where(gx > 0, 1, 0) + jnp.where(gx < nx - 1, 1, 0)
    beside_y = jnp.where(gy > 0, 1, 0) + jnp.where(gy < ny - 1, 1, 0)

    def greet(who):
        @pl.when(who)
        def _():
            pl.semaphore_wait(barrier, beside_x + beside_y + beside_x * beside_y)

    every = list(range(T))
    states = [(A, B, even, odd), (B, A, odd, even), (A, B, even, odd), (B, A, odd, None)]
    near = ((0, 0), (1, 0), (0, 1), (2, 0), (0, 2))

    def end(s, d):
        return d + s * (X - 1 - 2 * d)

    def lines_out(first_line, ref, xo, cells):
        for s, t in sides:
            for h in range(H):
                for i, (dx, dy) in enumerate(cells):
                    cs[s, t, pl.ds((first_line + i) * H + h, 1), :] = row(
                        ref, depth_x(s, dx), h, depth_y(t, dy), xo, PAD)

    def begin(s):
        first_w(end(s, 0), s)
        for d in range(1, quarter):
            first_w(end(s, d))

    def admit_ends(s):
        for d in range(quarter):
            admit(end(s, d), s if d < 2 else None, d + 1)

    loaded(("p", "q"), "ends")
    loop(2, begin, 2)
    loaded(("c",), "ends")
    loop(2, admit_ends, 2)
    lines_out(0, even, 1, near)
    lines_out(5, adm, OUT, near[:3])
    for s, t in sides:
        for h in range(H):
            x0[s, pl.ds(extra + t * H + h, 1), :] = row(even, depth_x(s, 1), h, depth_y(t, 0), 1, PAD)
            for i, d in enumerate((2, 1)):
                x0[s, pl.ds(extra + 2 * H * (i + 1) + t * H + h, 1), :] = row(
                    adm, depth_x(s, d), h, depth_y(t, 0), OUT, PAD)
    pending = [[] for _ in range(STEPS)]
    starts = []

    def both(make):
        held.clear()
        entry = make(None)
        held[0](late)
        starts.append(held[0])
        return entry

    greet(late)
    for s, t in sides:
        pending[0].append(both(lambda now: to_corner(
            s, t, cs.at[s, t, pl.ds(0, 16)], cr.at[1 - s, 1 - t, pl.ds(0, 16)], now)))
    second = []
    by_y = [[] for _ in range(STEPS)]

    def first_out(at, count, entries):
        for s in range(2):
            entries.append(both(lambda now: to_x(
                s, x0.at[s, pl.ds(at, count)], x0r.at[1 - s, pl.ds(at, count)], now)))

    first_out(0, extra + 16, pending[0])
    loaded(("o", "n"), "ends")
    for k in range(3):
        def narrow(s, k=k):
            for d in range(3 - k):
                alone(end(s, d), every, *states[k], fs.at[k, s] if d == 0 else None)

        loop(2, narrow, 2)
        if k < 2:
            lines_out(8 + 3 * k, states[k][3], 1, near[:3 if k == 0 else 1])
        if k == 1:
            for s, t in sides:
                pending[1].append(both(lambda now: to_corner(
                    s, t, cs.at[s, t, pl.ds(16, 8)], cr.at[1 - s, 1 - t, pl.ds(16, 8)], now)))
            first_out(extra + 16, H * Y, second)
        for layer in ((), (0, 1), (2,))[k]:
            for s in range(2):
                pending[layer + 1].append(both(lambda now: to_x(s, fs.at[layer, s], fr.at[layer, 1 - s], now)))

    loaded(("p", "q"), "middle")
    loop(X - 2 * quarter, lambda i: first_w(i + quarter), 4)
    loaded(("c",), "middle")
    loop(X - 2 * quarter, lambda i: admit(i + quarter), 4)
    flat_a = flat(adm)
    for t in range(2):
        for h in range(H):
            for s in range(2):
                ya[t, pl.ds(3 * H * X + s * H + h, 1), :] = cs[s, t, pl.ds(2 * H + h, 1), :]
                ya[t, pl.ds(3 * H * X + 2 * H + s * H + h, 1), :] = row(
                    adm, depth_x(s, 0), h, depth_y(t, 2), OUT, PAD)
            ya[t, pl.ds(h * X, X), :] = flat(even)[line(even, h, depth_y(t, 0), 1, PAD), :]
            for d in range(2):
                ya[t, pl.ds(((d + 1) * H + h) * X, X), :] = flat_a[line(adm, h, depth_y(t, d), OUT, PAD), :]
        for s in range(2):
            for h in range(H):
                for d in range(2):
                    ya[t, pl.ds(h * X + depth_x(s, d), 1), :] = cs[s, t, pl.ds(d * H + h, 1), :]
        by_y[0].append(both(lambda now: to_y(t, ya.at[t], yar.at[1 - t], now)))
    loaded(("o", "n"), "middle")
    for k in range(STEPS):
        done = 3 - k
        if k == STEPS - 1:
            loop(X, lambda x: alone(x, every, *states[k]), 4)
            break
        loop(X - 2 * done, lambda i: alone(i + done, every, *states[k]), (5, 6, 7)[k])
        for t in range(2):
            for h in range(H):
                dst = states[k][3]
                ys[k, t, h] = flat(dst)[line(dst, h, depth_y(t, 0), 1, PAD), :]
                for s in range(2):
                    if k < 2:
                        for d in range(2 - k):
                            ys[k, t, h, pl.ds(depth_x(s, d), 1), :] = (
                                fs[k, s, h, pl.ds(depth_y(t, 0), 1), :] if d == 0
                                else cs[s, t, pl.ds((8 + d) * H + h, 1), :])
            if k < 2:
                by_y[k + 1].append(both(lambda now: to_y(t, ys.at[k, t], yr.at[k, 1 - t], now)))
            else:
                by_y[k + 1].append(to_y(t, ys.at[k, t], yr.at[k, 1 - t], late | early))
        if k == 1:
            greet(early)
            for start in starts:
                start(early)

    def own_plane(k, s, h, at, size):
        return x0[s, pl.ds(h * Y + at, size), :] if k == 0 else fs[k - 1, s, h, pl.ds(at, size), :]

    def their_plane(k, s, h, at, size):
        return x0r[s, pl.ds(h * Y + at, size), :] if k == 0 else fr[k - 1, s, h, pl.ds(at, size), :]

    sub = lax.broadcasted_iota(jnp.int32, (8, LANES), 0)

    def row_beyond(k, x, h, j):
        at = {0: (0, False, 0), T - 1: (1, False, 7), -1: (0, True, 7), T: (1, True, 0)}.get(j)
        if at is None:
            return None
        t, own, r = at
        if k == 0:
            value = (ya if own else yar)[t, pl.ds(h * X + x, 1), :]
        else:
            value = (ys if own else yr)[k - 1, t, h, pl.ds(x, 1), :]
        return jnp.where(sub == r, jnp.broadcast_to(value, (8, LANES)), 0.0)

    def beyond(k, x, s=None, d=None):
        def value(h, j):
            total = None
            if d is None or d >= 0:
                total = row_beyond(k, x, h, j)
            if d in (0, -1) and 0 <= j < T:
                face = (their_plane if d == 0 else own_plane)(k, s, h, 8 * j, 8)
                total = face if total is None else total + face
            return total

        return value

    def sources(k, then, dst):
        def plane(s, d, value):
            x = depth_x(s, d) + OUT

            def part(j):
                for h in range(H):
                    add = adm[x, h, rows(j, PAD), :] * value(k, s, h, 8 * j, 8)
                    then[x, h, rows(j, WIDE), :] = then[x, h, rows(j, WIDE), :] + add
                    dst[x, h, rows(j, WIDE), :] = dst[x, h, rows(j, WIDE), :] + al * add

            loop(T, part, T)

        def cell(s, t, dx, dy, h, value):
            x, y = depth_x(s, dx) + OUT, depth_y(t, dy)
            add = adm[x, h, pl.ds(PAD + y, 1), :] * value
            at = pl.ds(WIDE + y, 1)
            then[x, h, at, :] = then[x, h, at, :] + add
            dst[x, h, at, :] = dst[x, h, at, :] + al * add

        if k == 0:
            for s in range(2):
                plane(s, 0, their_plane)
                plane(s, -1, own_plane)
        for s, t in sides:
            base = (0, 8, 11)[k]
            for h in range(H):
                def at(i):
                    return cr[s, t, pl.ds((base + i) * H + h, 1), :]

                cell(s, t, -1, 0, h, at(0))
                cell(s, t, 0, -1, h, at(0))
                if k < 2:
                    cell(s, t, -2, 0, h, at(1))
                    cell(s, t, 0, -2, h, at(2))
                    beside = their_plane(k, s, h, depth_y(t, 0), 1)
                    if k == 0:
                        beside = beside + yar[t, pl.ds(h * X + depth_x(s, 0), 1), :]
                    else:
                        beside = beside + yr[k - 1, t, h, pl.ds(depth_x(s, 0), 1), :]
                    cell(s, t, -1, -1, h, beside)
                if k == 0:
                    cell(s, t, -3, 0, h, at(3))
                    cell(s, t, 0, -3, h, at(4))
                    cell(s, t, -2, -1, h, x0r[s, pl.ds(extra + t * H + h, 1), :])
                    cell(s, t, -1, -2, h, yar[t, pl.ds(3 * H * X + s * H + h, 1), :])

    def put(s, t, dx, dy, h, value):
        adm[depth_x(s, dx) + OUT, h, pl.ds(PAD + depth_y(t, dy), 1), :] = value

    around = [-1, 0, T - 1, T]
    full = list(range(-1, T + 1))
    frames = {
        1: [(-2, every), (-1, full), (0, full), (1, full)],
        2: [(-1, every), (0, full), (1, full), (2, full)],
        3: [(0, every), (1, every), (2, every), (3, every)],
    }
    steps = [None] + [
        ((dB, dA) if k % 2 == 1 else (dA, dB)) + ((dD, dE) if k % 2 == 1 else (dE, dD)) for k in range(1, STEPS)]
    steps[STEPS - 1] = steps[STEPS - 1][:3] + (None,)

    for entry in by_y[0]:
        arrived(entry)
    for t in range(2):
        for h in range(H):
            for d in range(2):
                flat_a[line(adm, h, depth_y(t, -1 - d), OUT, PAD), :] = yar[t, pl.ds(((d + 1) * H + h) * X, X), :]
            for s in range(2):
                put(s, t, 0, -3, h, yar[t, pl.ds(3 * H * X + 2 * H + s * H + h, 1), :])

    def first_rows(x):
        for j in around:
            for h in range(H):
                add = adm[x + OUT, h, rows(j, PAD), :] * row_beyond(0, x, h, j)
                dB[x + OUT, h, rows(j, WIDE), :] = add
                dD[x + OUT, h, rows(j, WIDE), :] = al * add

    loop(X, first_rows, 4)
    for k in range(1, STEPS):
        inner = k + 1
        middle = around if k < STEPS - 1 else [0, T - 1]
        for entry in by_y[k]:
            arrived(entry)
        loop(X - 2 * inner, lambda i: coupled(
            i + inner, middle, *steps[k], k == 1, beyond(k, i + inner)), (0, 6, 5, 8)[k])

    def place(d):
        for s in range(2):
            def part(j, s=s):
                for h in range(H):
                    adm[depth_x(s, -1 - d) + OUT, h, rows(j, PAD), :] = x0r[
                        s, rows(j, ((d + 1) * H + h) * Y + 16 * d), :]

            loop(T, part, T)

    for entry in pending[0]:
        arrived(entry)
    place(0)
    for s, t in sides:
        for h in range(H):
            for i, d in enumerate((-3, -2)):
                put(s, t, d, 0, h, x0r[s, pl.ds(extra + 2 * H * (i + 1) + t * H + h, 1), :])
            for i, (dx, dy) in enumerate(near[:3]):
                put(s, t, -1 - dx, -1 - dy, h, cr[s, t, pl.ds((5 + i) * H + h, 1), :])
    sources(0, dB, dD)
    for k in range(1, STEPS):
        def near_face(s, touching, k=k):
            for d, tiles in frames[k]:
                if (d in (0, -1)) == touching:
                    coupled(end(s, d), tiles, *steps[k], k == 1, beyond(k, end(s, d), s, d))

        if k == 1:
            for entry in second:
                arrived(entry)
            place(1)
        loop(2, lambda s: near_face(s, False), 2)
        for entry in pending[k]:
            arrived(entry)
        loop(2, lambda s: near_face(s, True), 2)
        if k < STEPS - 1:
            sources(k, steps[k][1], steps[k][3])

    for at, (size, ok) in enumerate(in_flight):
        @pl.when(ok)
        def _():
            whole = flat(dE).at[pl.ds(0, size)]
            pltpu.make_async_copy(whole, whole, send_sem.at[at]).wait()


def store_kernel(a, b, o, n, p_out, q_out, o_out, n_out, sems):
    pairs = ((a, p_out), (b, q_out), (o, o_out), (n, n_out))
    for at, (src, dst) in enumerate(pairs):
        for h in range(2):
            pltpu.make_async_copy(src.at[:, h], dst.at[:, :, pl.ds(LANES * h, LANES)], sems.at[at]).start()
    for at, (src, dst) in enumerate(pairs):
        pltpu.make_async_copy(src, src, sems.at[at]).wait()


def per_device(nx, ny, pressure, previous, oxygen_aux, nitrogen_aux, cell_class, wall_admittance, medium):
    X, Y, Z = pressure.shape
    H = Z // LANES
    split = (X, H, Y, LANES)
    padded = (X + 2, H, Y + 2 * PAD, LANES)
    wide = (X + 2 * OUT, H, Y + 2 * WIDE, LANES)
    hbm = pl.BlockSpec(memory_space=pl.ANY)
    vmem = pl.BlockSpec(memory_space=pltpu.VMEM)
    smem = pl.BlockSpec(memory_space=pltpu.SMEM)
    f32 = jnp.float32
    rows_y = 3 * H * X + 8
    state = pl.pallas_call(
        functools.partial(steps_kernel, nx, ny),
        out_shape=[pltpu.VMEM(split, f32)] * 4,
        in_specs=[hbm] * 5 + [smem] * 2,
        out_specs=[vmem] * 4,
        scratch_shapes=[
            pltpu.VMEM(split, jnp.int32),
            pltpu.VMEM((X + 2 * OUT, H, Y + 2 * PAD, LANES), f32),
            pltpu.VMEM(padded, f32),
            pltpu.VMEM(padded, f32),
            *[pltpu.VMEM(wide, f32)] * 6,
            pltpu.VMEM((2, 3 * H * Y + 16, LANES), f32),
            pltpu.VMEM((STEPS - 1, 2, H, Y, LANES), f32),
            pltpu.VMEM((STEPS - 1, 2, H, X, LANES), f32),
            pltpu.VMEM((2, rows_y, LANES), f32),
            pltpu.VMEM((2, 2, 24, LANES), f32),
            pltpu.VMEM((2, 3 * H * Y + 16, LANES), f32),
            pltpu.VMEM((STEPS - 1, 2, H, Y, LANES), f32),
            pltpu.VMEM((STEPS - 1, 2, H, X, LANES), f32),
            pltpu.VMEM((2, rows_y, LANES), f32),
            pltpu.VMEM((2, 2, 24, LANES), f32),
            pltpu.SemaphoreType.DMA((6,)),
            pltpu.SemaphoreType.DMA((8,)),
            pltpu.SemaphoreType.DMA((26,)),
        ],
        compiler_params=pltpu.CompilerParams(
            collective_id=0, has_side_effects=True, vmem_limit_bytes=56 << 20),
    )(pressure, previous, oxygen_aux, nitrogen_aux, cell_class, wall_admittance, medium)
    out = pl.pallas_call(
        store_kernel,
        out_shape=[jax.ShapeDtypeStruct((X, Y, Z), f32)] * 4,
        in_specs=[vmem] * 4,
        out_specs=[hbm] * 4,
        scratch_shapes=[pltpu.SemaphoreType.DMA((4,))],
        compiler_params=pltpu.CompilerParams(vmem_limit_bytes=16 << 20),
    )(*state)
    return tuple(out)


def solution(mesh):
    field = P("gx", "gy", None)
    return jax.shard_map(
        functools.partial(per_device, mesh.shape["gx"], mesh.shape["gy"]),
        mesh=mesh,
        in_specs=(field,) * 5 + (P(), P()),
        out_specs=(field,) * 4,
        check_vma=False,
    )
```

```python
import functools

import jax
import jax.numpy as jnp
from jax import lax
from jax.experimental import pallas as pl
from jax.experimental.pallas import tpu as pltpu
from jax.sharding import PartitionSpec as P

STEPS = 4
NCLASS = 8
MESH = pl.DeviceIdType.MESH
LANES = 128
PAD = 8
WIDE = 16
OUT = 3


def steps_kernel(nx, ny, p_hbm, q_hbm, o_hbm, n_hbm, c_hbm, wall, medium, A, B, O, N,
                 cls, adm, even, odd, dA, dB, dO, dN, dE, dD,
                 x0, fs, ys, ya, cs, x0r, fr, yr, yar, cr,
                 load_sem, send_sem, recv_sem):
    X, H, Y, _ = A.shape
    T = Y // 8
    gx, gy = lax.axis_index("gx"), lax.axis_index("gy")
    xs = (lax.rem(gx + nx - 1, nx), lax.rem(gx + 1, nx))
    yside = (lax.rem(gy + ny - 1, ny), lax.rem(gy + 1, ny))
    there_x = (gx > 0, gx < nx - 1)
    there_y = (gy > 0, gy < ny - 1)
    sides = [(s, t) for s in range(2) for t in range(2)]

    barrier = pltpu.get_barrier_semaphore()
    others = [((xs[s], gy), there_x[s]) for s in range(2)]
    others += [((gx, yside[t]), there_y[t]) for t in range(2)]
    others += [((xs[s], yside[t]), there_x[s] & there_y[t]) for s, t in sides]
    for other, ok in others[::-1]:
        @pl.when(ok)
        def _():
            pl.semaphore_signal(barrier, inc=1, device_id=other, device_id_type=MESH)

    quarter = X // 4
    chunks = {"ends": ((0, quarter), (X - quarter, quarter)), "middle": ((quarter, X - 2 * quarter),)}
    groups = (("p", "q"), ("c",), ("o", "n"))
    source = {"p": (p_hbm, A), "q": (q_hbm, B), "c": (c_hbm, cls), "o": (o_hbm, O), "n": (n_hbm, N)}
    order = [(names, part) for part in ("ends", "middle") for names in groups]
    for at, (names, part) in enumerate(order):
        for name in names:
            src, dst = source[name]
            for x, count in chunks[part]:
                for h in range(H):
                    pltpu.make_async_copy(
                        src.at[pl.ds(x, count), :, pl.ds(LANES * h, LANES)],
                        dst.at[pl.ds(x, count), h], load_sem.at[at]).start()

    def loaded(names, part):
        planes = len(names) * sum(count for _, count in chunks[part])
        whole = A.at[pl.ds(0, planes)]
        pltpu.make_async_copy(whole, whole, load_sem.at[order.index((names, part))]).wait()

    m0, m1, m2, m3 = medium[0], medium[1], medium[2], medium[3]
    c = 0.05 * medium[4]
    al = 0.33 + c

    lane = lax.broadcasted_iota(jnp.int32, (8, LANES), 1)
    first, last = lane == 0, lane == LANES - 1
    zero = jnp.zeros((8, LANES), jnp.float32)

    def loop(count, body, unroll=1):
        lax.fori_loop(0, count, lambda i, carry: (body(i), carry)[1], 0, unroll=unroll)

    def rows(j, pad=0, by=0):
        return pl.ds(pad + 8 * j + by, 8)

    def depth_x(s, d):
        return d if s == 0 else X - 1 - d

    def depth_y(t, d):
        return d if t == 0 else Y - 1 - d

    def advance(x, j, now, then, oxy, nit, xo, pad, src, wx, wpad, fresh=False, across=None):
        w = [src[x + wx, h, rows(j, wpad), :] for h in range(H)]
        down = [pltpu.roll(v, 1, 1) for v in w]
        up = [pltpu.roll(v, LANES - 1, 1) for v in w]
        below = [jnp.where(first, 0.0, down[0]), jnp.where(first, down[0], down[1])]
        above = [jnp.where(last, up[1], up[0]), jnp.where(last, 0.0, up[1])]
        result = []
        for h in range(H):
            at = (x + xo, h, rows(j, pad), slice(None))
            p = now[at]
            total = src[x + wx - 1, h, rows(j, wpad), :] + src[x + wx + 1, h, rows(j, wpad), :]
            total = total + (src[x + wx, h, rows(j, wpad, -1), :] + src[x + wx, h, rows(j, wpad, 1), :])
            total = total + (below[h] + above[h])
            beyond = across(h, j) if across is not None else None
            if beyond is not None:
                total = total + beyond
            a = adm[x + OUT, h, rows(j, PAD), :]
            if fresh:
                o, n = m1 * p, m3 * p
                new = a * ((total - 6.0 * w[h]) + (2.0 * p - (o + n)))
            else:
                q = then[at]
                d = p - q
                o = m0 * oxy[at] + m1 * d
                n = m2 * nit[at] + m3 * d
                new = q + a * ((total - 6.0 * w[h]) + (2.0 * d - (o + n)))
            result.append((h, at, p, new, o, n))
        return result

    def alone(x, tiles, now, then, src, dst, keep=None):
        for j0 in range(0, len(tiles), 2):
            done = [(j, r) for j in tiles[j0:j0 + 2] for r in advance(x, j, now, then, O, N, 0, 0, src, 1, PAD)]
            for j, (h, at, p, new, o, n) in done:
                then[at] = new
                O[at] = o
                N[at] = n
                if dst is not None:
                    v = al * new - c * p
                    dst[x + 1, h, rows(j, PAD), :] = v
                    if keep is not None:
                        keep[h, rows(j), :] = v

    def coupled(x, tiles, now, then, src, dst, fresh, across=None):
        for j0 in range(0, len(tiles), 2):
            done = [(j, r) for j in tiles[j0:j0 + 2]
                    for r in advance(x, j, now, then, dO, dN, OUT, WIDE, src, OUT, WIDE, fresh, across)]
            for j, (h, at, p, new, o, n) in done:
                if dst is not None:
                    then[at] = new
                    dO[at] = o
                    dN[at] = n
                    dst[at] = al * new - c * p
                else:
                    to = (x, h, rows(j), slice(None))
                    A[to] = A[to] + new
                    B[to] = B[to] + p
                    O[to] = O[to] + o
                    N[to] = N[to] + n

    def flat(ref):
        planes, halves, height, _ = ref.shape
        return ref.reshape(planes * halves * height, LANES)

    def line(ref, h, y, xo, pad):
        height = ref.shape[2]
        return pl.ds((xo * H + h) * height + pad + y, X, stride=H * height)

    messages = iter(range(recv_sem.shape[0]))
    in_flight = [[0, ok] for _, ok in others]

    def send(group, src, dst, device, ok, back, now):
        at = next(messages)
        in_flight[group][0] += src.size // LANES

        def describe():
            return pltpu.make_async_remote_copy(
                src_ref=src, dst_ref=dst, send_sem=send_sem.at[group], recv_sem=recv_sem.at[at],
                device_id=device, device_id_type=MESH)

        def start(when):
            @pl.when(ok & when)
            def _():
                describe().start()

        if now is None:
            held.append(start)
        else:
            start(now)
        return describe, back

    def arrived(entry):
        @pl.when(entry[1])
        def _():
            entry[0]().wait_recv()

    def clear(x):
        for ref in (dE, dD, dB):
            for h in range(H):
                for j in range(-2, T + 2):
                    ref[x, h, rows(j, WIDE), :] = zero
        for h in range(H):
            adm[x, h, rows(-1, PAD), :] = zero
            adm[x, h, rows(T, PAD), :] = zero

    def clear_next(i):
        for d in (2, 3):
            for ref in (dA, dO, dN):
                for h in range(H):
                    for j in range(T):
                        ref[d + i * (X - 1 - 2 * d) + OUT, h, rows(j, WIDE), :] = zero

    def clear_own(x):
        for h in range(H):
            for ref in (even, odd):
                ref[x, h, rows(-1, PAD), :] = zero
                ref[x, h, rows(T, PAD), :] = zero

    def clear_faces(j):
        for h in range(H):
            for ref in (even, odd):
                for x in (0, X + 1):
                    ref[x, h, rows(j, PAD), :] = zero
            for x in (0, X + 2 * OUT - 1):
                adm[x, h, rows(j, PAD), :] = zero

    loop(X + 2 * OUT, clear)
    loop(2, clear_next)
    loop(X + 2, clear_own)
    loop(T, clear_faces)
    blank = jnp.zeros((X, LANES), jnp.float32)
    for s in range(2):
        @pl.when(jnp.logical_not(there_x[s]))
        def _():
            def none(j):
                for h in range(H):
                    for k in range(STEPS - 1):
                        fr[k, s, h, rows(j), :] = zero

            def none_first(i):
                x0r[s, pl.ds(8 * i, 8), :] = zero

            loop(T, none)
            loop(x0.shape[1] // 8, none_first, 5)

        @pl.when(jnp.logical_not(there_y[s]))
        def _():
            for h in range(H):
                for k in range(STEPS - 1):
                    yr[k, s, h] = blank
                for f in range(3):
                    yar[s, pl.ds((f * H + h) * X, X), :] = blank
            yar[s, pl.ds(3 * H * X, 8), :] = zero

        for t in range(2):
            @pl.when(jnp.logical_not(there_x[s] & there_y[t]))
            def _():
                for i in range(3):
                    cr[s, t, pl.ds(8 * i, 8), :] = zero

    def first_w(x, keep=None):
        for j in range(T):
            for h in range(H):
                v = al * A[x, h, rows(j), :] - c * B[x, h, rows(j), :]
                even[x + 1, h, rows(j, PAD), :] = v
                if keep is not None:
                    x0[keep, rows(j, h * Y), :] = v

    extra = 2 * H * Y
    table = [1.0 / (1.0 + 0.5 * jnp.full((8, LANES), wall[k], jnp.float32)) for k in range(1, NCLASS)]

    def admit(x, keep=None, field=0):
        for j in range(T):
            for h in range(H):
                kind = cls[x, h, rows(j), :]
                a = jnp.ones((8, LANES), jnp.float32)
                for k in range(1, NCLASS):
                    a = jnp.where(kind == k, table[k - 1], a)
                adm[x + OUT, h, rows(j, PAD), :] = a
                if keep is not None:
                    x0[keep, rows(j, (field * H + h) * Y + (16 if field == 2 else 0)), :] = a

    def row(ref, x, h, y, xo, pad):
        return ref[x + xo, h, pl.ds(pad + y, 1), :]

    def to_x(s, src, dst, now):
        return send(s, src, dst, (xs[s], gy), there_x[s], there_x[1 - s], now)

    def to_y(t, src, dst, now):
        return send(2 + t, src, dst, (gx, yside[t]), there_y[t], there_y[1 - t], now)

    def to_corner(s, t, src, dst, now):
        return send(4 + 2 * s + t, src, dst, (xs[s], yside[t]), there_x[s] & there_y[t],
                    there_x[1 - s] & there_y[1 - t], now)

    ring = max(nx // 4, 1)
    early = (lax.rem(gx, ring) == 0) & (gx > 0)
    late = jnp.logical_not(early)
    held = []

    beside_x = jnp.where(gx > 0, 1, 0) + jnp.where(gx < nx - 1, 1, 0)
    beside_y = jnp.where(gy > 0, 1, 0) + jnp.where(gy < ny - 1, 1, 0)

    def greet(who):
        @pl.when(who)
        def _():
            pl.semaphore_wait(barrier, beside_x + beside_y + beside_x * beside_y)

    every = list(range(T))
    states = [(A, B, even, odd), (B, A, odd, even), (A, B, even, odd), (B, A, odd, None)]
    near = ((0, 0), (1, 0), (0, 1), (2, 0), (0, 2))

    def end(s, d):
        return d + s * (X - 1 - 2 * d)

    def lines_out(first_line, ref, xo, cells):
        for s, t in sides:
            for h in range(H):
                for i, (dx, dy) in enumerate(cells):
                    cs[s, t, pl.ds((first_line + i) * H + h, 1), :] = row(
                        ref, depth_x(s, dx), h, depth_y(t, dy), xo, PAD)

    def begin(s):
        first_w(end(s, 0), s)
        for d in range(1, quarter):
            first_w(end(s, d))

    def admit_ends(s):
        for d in range(quarter):
            admit(end(s, d), s if d < 2 else None, d + 1)

    loaded(("p", "q"), "ends")
    loop(2, begin, 2)
    loaded(("c",), "ends")
    loop(2, admit_ends, 2)
    lines_out(0, even, 1, near)
    lines_out(5, adm, OUT, near[:3])
    for s, t in sides:
        for h in range(H):
            x0[s, pl.ds(extra + t * H + h, 1), :] = row(even, depth_x(s, 1), h, depth_y(t, 0), 1, PAD)
            for i, d in enumerate((2, 1)):
                x0[s, pl.ds(extra + 2 * H * (i + 1) + t * H + h, 1), :] = row(
                    adm, depth_x(s, d), h, depth_y(t, 0), OUT, PAD)
    pending = [[] for _ in range(STEPS)]
    starts = []

    def both(make):
        held.clear()
        entry = make(None)
        held[0](late)
        starts.append(held[0])
        return entry

    greet(late)
    for s, t in sides:
        pending[0].append(both(lambda now: to_corner(
            s, t, cs.at[s, t, pl.ds(0, 16)], cr.at[1 - s, 1 - t, pl.ds(0, 16)], now)))
    second = []
    by_y = [[] for _ in range(STEPS)]

    def first_out(at, count, entries):
        for s in range(2):
            entries.append(both(lambda now: to_x(
                s, x0.at[s, pl.ds(at, count)], x0r.at[1 - s, pl.ds(at, count)], now)))

    first_out(0, extra + 16, pending[0])
    loaded(("o", "n"), "ends")
    for k in range(3):
        def narrow(s, k=k):
            for d in range(3 - k):
                alone(end(s, d), every, *states[k], fs.at[k, s] if d == 0 else None)

        loop(2, narrow, 2)
        if k < 2:
            lines_out(8 + 3 * k, states[k][3], 1, near[:3 if k == 0 else 1])
        if k == 1:
            for s, t in sides:
                pending[1].append(both(lambda now: to_corner(
                    s, t, cs.at[s, t, pl.ds(16, 8)], cr.at[1 - s, 1 - t, pl.ds(16, 8)], now)))
            first_out(extra + 16, H * Y, second)
        for layer in ((), (0, 1), (2,))[k]:
            for s in range(2):
                pending[layer + 1].append(both(lambda now: to_x(s, fs.at[layer, s], fr.at[layer, 1 - s], now)))

    loaded(("p", "q"), "middle")
    loop(X - 2 * quarter, lambda i: first_w(i + quarter), 4)
    loaded(("c",), "middle")
    loop(X - 2 * quarter, lambda i: admit(i + quarter), 4)
    flat_a = flat(adm)
    for t in range(2):
        for h in range(H):
            for s in range(2):
                ya[t, pl.ds(3 * H * X + s * H + h, 1), :] = cs[s, t, pl.ds(2 * H + h, 1), :]
                ya[t, pl.ds(3 * H * X + 2 * H + s * H + h, 1), :] = row(
                    adm, depth_x(s, 0), h, depth_y(t, 2), OUT, PAD)
            ya[t, pl.ds(h * X, X), :] = flat(even)[line(even, h, depth_y(t, 0), 1, PAD), :]
            for d in range(2):
                ya[t, pl.ds(((d + 1) * H + h) * X, X), :] = flat_a[line(adm, h, depth_y(t, d), OUT, PAD), :]
        for s in range(2):
            for h in range(H):
                for d in range(2):
                    ya[t, pl.ds(h * X + depth_x(s, d), 1), :] = cs[s, t, pl.ds(d * H + h, 1), :]
        by_y[0].append(both(lambda now: to_y(t, ya.at[t], yar.at[1 - t], now)))
    loaded(("o", "n"), "middle")
    for k in range(STEPS):
        done = 3 - k
        if k == STEPS - 1:
            loop(X, lambda x: alone(x, every, *states[k]), 4)
            break
        loop(X - 2 * done, lambda i: alone(i + done, every, *states[k]), (5, 6, 7)[k])
        for t in range(2):
            for h in range(H):
                dst = states[k][3]
                ys[k, t, h] = flat(dst)[line(dst, h, depth_y(t, 0), 1, PAD), :]
                for s in range(2):
                    if k < 2:
                        for d in range(2 - k):
                            ys[k, t, h, pl.ds(depth_x(s, d), 1), :] = (
                                fs[k, s, h, pl.ds(depth_y(t, 0), 1), :] if d == 0
                                else cs[s, t, pl.ds((8 + d) * H + h, 1), :])
            if k < 2:
                by_y[k + 1].append(both(lambda now: to_y(t, ys.at[k, t], yr.at[k, 1 - t], now)))
            else:
                by_y[k + 1].append(to_y(t, ys.at[k, t], yr.at[k, 1 - t], late | early))
        if k == 1:
            greet(early)
            for start in starts:
                start(early)

    def own_plane(k, s, h, at, size):
        return x0[s, pl.ds(h * Y + at, size), :] if k == 0 else fs[k - 1, s, h, pl.ds(at, size), :]

    def their_plane(k, s, h, at, size):
        return x0r[s, pl.ds(h * Y + at, size), :] if k == 0 else fr[k - 1, s, h, pl.ds(at, size), :]

    sub = lax.broadcasted_iota(jnp.int32, (8, LANES), 0)

    def row_beyond(k, x, h, j):
        at = {0: (0, False, 0), T - 1: (1, False, 7), -1: (0, True, 7), T: (1, True, 0)}.get(j)
        if at is None:
            return None
        t, own, r = at
        if k == 0:
            value = (ya if own else yar)[t, pl.ds(h * X + x, 1), :]
        else:
            value = (ys if own else yr)[k - 1, t, h, pl.ds(x, 1), :]
        return jnp.where(sub == r, jnp.broadcast_to(value, (8, LANES)), 0.0)

    def beyond(k, x, s=None, d=None):
        def value(h, j):
            total = None
            if d is None or d >= 0:
                total = row_beyond(k, x, h, j)
            if d in (0, -1) and 0 <= j < T and k < STEPS - 1:
                face = (their_plane if d == 0 else own_plane)(k, s, h, 8 * j, 8)
                total = face if total is None else total + face
            return total

        return value

    def sources(k, then, dst):
        def plane(s, d, value):
            x = depth_x(s, d) + OUT

            def part(j):
                for h in range(H):
                    add = adm[x, h, rows(j, PAD), :] * value(k, s, h, 8 * j, 8)
                    then[x, h, rows(j, WIDE), :] = then[x, h, rows(j, WIDE), :] + add
                    dst[x, h, rows(j, WIDE), :] = dst[x, h, rows(j, WIDE), :] + al * add

            loop(T, part, T)

        def cell(s, t, dx, dy, h, value):
            x, y = depth_x(s, dx) + OUT, depth_y(t, dy)
            add = adm[x, h, pl.ds(PAD + y, 1), :] * value
            at = pl.ds(WIDE + y, 1)
            then[x, h, at, :] = then[x, h, at, :] + add
            dst[x, h, at, :] = dst[x, h, at, :] + al * add

        if k == 0:
            for s in range(2):
                plane(s, 0, their_plane)
                plane(s, -1, own_plane)
        for s, t in sides:
            base = (0, 8, 11)[k]
            for h in range(H):
                def at(i):
                    return cr[s, t, pl.ds((base + i) * H + h, 1), :]

                cell(s, t, -1, 0, h, at(0))
                cell(s, t, 0, -1, h, at(0))
                if k < 2:
                    cell(s, t, -2, 0, h, at(1))
                    cell(s, t, 0, -2, h, at(2))
                    beside = their_plane(k, s, h, depth_y(t, 0), 1)
                    if k == 0:
                        beside = beside + yar[t, pl.ds(h * X + depth_x(s, 0), 1), :]
                    else:
                        beside = beside + yr[k - 1, t, h, pl.ds(depth_x(s, 0), 1), :]
                    cell(s, t, -1, -1, h, beside)
                if k == 0:
                    cell(s, t, -3, 0, h, at(3))
                    cell(s, t, 0, -3, h, at(4))
                    cell(s, t, -2, -1, h, x0r[s, pl.ds(extra + t * H + h, 1), :])
                    cell(s, t, -1, -2, h, yar[t, pl.ds(3 * H * X + s * H + h, 1), :])

    def put(s, t, dx, dy, h, value):
        adm[depth_x(s, dx) + OUT, h, pl.ds(PAD + depth_y(t, dy), 1), :] = value

    around = [-1, 0, T - 1, T]
    full = list(range(-1, T + 1))
    frames = {
        1: [(-2, every), (-1, full), (0, full), (1, full)],
        2: [(-1, every), (0, full), (1, full), (2, full)],
        3: [(0, every), (1, every), (2, every), (3, every)],
    }
    steps = [None] + [
        ((dB, dA) if k % 2 == 1 else (dA, dB)) + ((dD, dE) if k % 2 == 1 else (dE, dD)) for k in range(1, STEPS)]
    steps[STEPS - 1] = steps[STEPS - 1][:3] + (None,)

    for entry in by_y[0]:
        arrived(entry)
    for t in range(2):
        for h in range(H):
            for d in range(2):
                flat_a[line(adm, h, depth_y(t, -1 - d), OUT, PAD), :] = yar[t, pl.ds(((d + 1) * H + h) * X, X), :]
            for s in range(2):
                put(s, t, 0, -3, h, yar[t, pl.ds(3 * H * X + 2 * H + s * H + h, 1), :])

    def first_rows(x):
        for j in around:
            for h in range(H):
                add = adm[x + OUT, h, rows(j, PAD), :] * row_beyond(0, x, h, j)
                dB[x + OUT, h, rows(j, WIDE), :] = add
                dD[x + OUT, h, rows(j, WIDE), :] = al * add

    loop(X, first_rows, 4)
    for k in range(1, STEPS):
        inner = k + 1
        middle = around if k < STEPS - 1 else [0, T - 1]
        for entry in by_y[k]:
            arrived(entry)
        loop(X - 2 * inner, lambda i: coupled(
            i + inner, middle, *steps[k], k == 1, beyond(k, i + inner)), (0, 6, 5, 8)[k])

    def place(d):
        for s in range(2):
            def part(j, s=s):
                for h in range(H):
                    adm[depth_x(s, -1 - d) + OUT, h, rows(j, PAD), :] = x0r[
                        s, rows(j, ((d + 1) * H + h) * Y + 16 * d), :]

            loop(T, part, T)

    for entry in pending[0]:
        arrived(entry)
    place(0)
    for s, t in sides:
        for h in range(H):
            for i, d in enumerate((-3, -2)):
                put(s, t, d, 0, h, x0r[s, pl.ds(extra + 2 * H * (i + 1) + t * H + h, 1), :])
            for i, (dx, dy) in enumerate(near[:3]):
                put(s, t, -1 - dx, -1 - dy, h, cr[s, t, pl.ds((5 + i) * H + h, 1), :])
    sources(0, dB, dD)
    for k in range(1, STEPS):
        def near_face(s, touching, k=k):
            for d, tiles in frames[k]:
                if (d in (0, -1) and k < STEPS - 1) == touching:
                    coupled(end(s, d), tiles, *steps[k], k == 1, beyond(k, end(s, d), s, d))

        if k == 1:
            for entry in second:
                arrived(entry)
            place(1)
        loop(2, lambda s: near_face(s, False), 2)
        for entry in pending[k]:
            arrived(entry)
        if k < STEPS - 1:
            loop(2, lambda s: near_face(s, True), 2)
            sources(k, steps[k][1], steps[k][3])

    for s in range(2):
        x = depth_x(s, 0)
        for j in range(T):
            for h in range(H):
                A[x, h, rows(j), :] = A[x, h, rows(j), :] + (
                    adm[x + OUT, h, rows(j, PAD), :] * their_plane(STEPS - 1, s, h, 8 * j, 8))

    for at, (size, ok) in enumerate(in_flight):
        @pl.when(ok)
        def _():
            whole = flat(dE).at[pl.ds(0, size)]
            pltpu.make_async_copy(whole, whole, send_sem.at[at]).wait()


def store_kernel(a, b, o, n, p_out, q_out, o_out, n_out, sems):
    pairs = ((a, p_out), (b, q_out), (o, o_out), (n, n_out))
    for at, (src, dst) in enumerate(pairs):
        for h in range(2):
            pltpu.make_async_copy(src.at[:, h], dst.at[:, :, pl.ds(LANES * h, LANES)], sems.at[at]).start()
    for at, (src, dst) in enumerate(pairs):
        pltpu.make_async_copy(src, src, sems.at[at]).wait()


def per_device(nx, ny, pressure, previous, oxygen_aux, nitrogen_aux, cell_class, wall_admittance, medium):
    X, Y, Z = pressure.shape
    H = Z // LANES
    split = (X, H, Y, LANES)
    padded = (X + 2, H, Y + 2 * PAD, LANES)
    wide = (X + 2 * OUT, H, Y + 2 * WIDE, LANES)
    hbm = pl.BlockSpec(memory_space=pl.ANY)
    vmem = pl.BlockSpec(memory_space=pltpu.VMEM)
    smem = pl.BlockSpec(memory_space=pltpu.SMEM)
    f32 = jnp.float32
    rows_y = 3 * H * X + 8
    state = pl.pallas_call(
        functools.partial(steps_kernel, nx, ny),
        out_shape=[pltpu.VMEM(split, f32)] * 4,
        in_specs=[hbm] * 5 + [smem] * 2,
        out_specs=[vmem] * 4,
        scratch_shapes=[
            pltpu.VMEM(split, jnp.int32),
            pltpu.VMEM((X + 2 * OUT, H, Y + 2 * PAD, LANES), f32),
            pltpu.VMEM(padded, f32),
            pltpu.VMEM(padded, f32),
            *[pltpu.VMEM(wide, f32)] * 6,
            pltpu.VMEM((2, 3 * H * Y + 16, LANES), f32),
            pltpu.VMEM((STEPS - 1, 2, H, Y, LANES), f32),
            pltpu.VMEM((STEPS - 1, 2, H, X, LANES), f32),
            pltpu.VMEM((2, rows_y, LANES), f32),
            pltpu.VMEM((2, 2, 24, LANES), f32),
            pltpu.VMEM((2, 3 * H * Y + 16, LANES), f32),
            pltpu.VMEM((STEPS - 1, 2, H, Y, LANES), f32),
            pltpu.VMEM((STEPS - 1, 2, H, X, LANES), f32),
            pltpu.VMEM((2, rows_y, LANES), f32),
            pltpu.VMEM((2, 2, 24, LANES), f32),
            pltpu.SemaphoreType.DMA((6,)),
            pltpu.SemaphoreType.DMA((8,)),
            pltpu.SemaphoreType.DMA((26,)),
        ],
        compiler_params=pltpu.CompilerParams(
            collective_id=0, has_side_effects=True, vmem_limit_bytes=56 << 20),
    )(pressure, previous, oxygen_aux, nitrogen_aux, cell_class, wall_admittance, medium)
    out = pl.pallas_call(
        store_kernel,
        out_shape=[jax.ShapeDtypeStruct((X, Y, Z), f32)] * 4,
        in_specs=[vmem] * 4,
        out_specs=[hbm] * 4,
        scratch_shapes=[pltpu.SemaphoreType.DMA((4,))],
        compiler_params=pltpu.CompilerParams(vmem_limit_bytes=16 << 20),
    )(*state)
    return tuple(out)


def solution(mesh):
    field = P("gx", "gy", None)
    return jax.shard_map(
        functools.partial(per_device, mesh.shape["gx"], mesh.shape["gy"]),
        mesh=mesh,
        in_specs=(field,) * 5 + (P(), P()),
        out_specs=(field,) * 4,
        check_vma=False,
    )
```
